256 devices in a mesh: dp: 32 (over z_lo, x, y), ctx: 8 (over z_hi, core).
Axes of the slice: x: 4, y: 4, z: 8 (z_hi: 4, z_lo: 2; z = z_hi * 2 + z_lo), core: 2. Of those that a mesh axis runs over, the one named last changes fastest.
Arguments:
- tokens: bfloat16 [2, 32768, 576], P(None, ('dp', 'ctx')), may hold values from -6 to 6
- lengths: int32 [2, 32, 4], P(None, 'dp'), may hold values from 1 to 1021, as said below
- gain_attn: bfloat16 [576], P('dp'), may hold values from 0.25 to 1.75
- w_query: bfloat16 [576, 576], P('dp', 'ctx'), may hold values from -0.25 to 0.25
- w_key: bfloat16 [576, 192], P('dp', 'ctx'), may hold values from -0.25 to 0.25
- w_value: bfloat16 [576, 192], P('dp', 'ctx'), may hold values from -0.25 to 0.25
- w_out: bfloat16 [576, 576], P('dp', 'ctx'), may hold values from -3.5 to 3.5
- gain_ffn: bfloat16 [576], P('dp'), may hold values from 0.25 to 1.75
- w_gate: bfloat16 [576, 1536], P('dp', 'ctx'), may hold values from -0.25 to 0.25
- w_up: bfloat16 [576, 1536], P('dp', 'ctx'), may hold values from -0.25 to 0.25
- w_down: bfloat16 [1536, 576], P('dp', 'ctx'), may hold values from -0.15625 to 0.15625
- cotangent: bfloat16 [2, 32768, 576], P(None, ('dp', 'ctx')), may hold values from -6 to 6
Outputs:
- block_out: bfloat16 [2, 32768, 576], P(None, ('dp', 'ctx'))
- d_tokens: float32 [2, 32768, 576], P(None, ('dp', 'ctx'))
- grad_gain_attn: float32 [576], P('dp')
- grad_query: float32 [576, 576], P('dp', 'ctx')
- grad_key: float32 [576, 192], P('dp', 'ctx')
- grad_value: float32 [576, 192], P('dp', 'ctx')
- grad_out: float32 [576, 576], P('dp', 'ctx')
- grad_gain_ffn: float32 [576], P('dp')
- grad_gate: float32 [576, 1536], P('dp', 'ctx')
- grad_up: float32 [576, 1536], P('dp', 'ctx')
- grad_down: float32 [1536, 576], P('dp', 'ctx')
The draws below stay inside these ranges and needn't reach their ends.
Inputs may be any that keep to these rules, and one draw needn't show every extreme that they name: The 4 lengths of each row sum to 1024; one of them, at a place drawn from the seed, is longer than 896. In the first row of the first micro-batch the other documents have one token each.
All inputs are finite; a program needn't handle non-finite values.
Results may differ from the reference program's by a relative error of at most 0.03.
Values may be sent and summed in bfloat16 or wider, within the bound.
No kernel may reach another device: no remote copies, remote signals or barrier semaphores. Data moves between devices by JAX's collectives and lax.ppermute only.
A program may use at most 128 MiB of HBM per device.

```python
import jax
import jax.numpy as jnp
from jax import lax

D = 576
FF = 1536
HEADS = 9
KV_HEADS = 3
HEAD = 64
MICRO = 2
NDOC = 4
QD = 576
KVD = 192
GROUP = 1024
STRETCH = 128
ROWS = 32768
N_DP = 32


def draw_lengths(key, part):
    key = jax.random.fold_in(key, 7)
    first_key, second_key, third_key = jax.random.split(key, 3)
    row_groups = ROWS // GROUP
    rest = jax.random.randint(first_key, (MICRO, row_groups), NDOC - 1, STRETCH)
    rest = rest.at[0, 0].set(NDOC - 1)
    spare = rest - (NDOC - 1)
    cuts = jax.random.randint(second_key, (MICRO, row_groups, NDOC - 2), 0, spare[..., None] + 1)
    cuts = jnp.sort(cuts, axis=-1)
    edges = jnp.concatenate([jnp.zeros((MICRO, row_groups, 1), jnp.int32), cuts, spare[..., None]], axis=-1)
    short_docs = edges[..., 1:] - edges[..., :-1] + 1
    filler = jnp.zeros((MICRO, row_groups, 1), jnp.int32)
    padded_after = jnp.concatenate([short_docs, filler], axis=-1)
    padded_before = jnp.concatenate([filler, short_docs], axis=-1)
    place = jax.random.randint(third_key, (MICRO, row_groups, 1), 0, NDOC)
    slots = jnp.arange(NDOC, dtype=jnp.int32)[None, None, :]
    long_doc = (GROUP - rest)[..., None]
    result = jnp.where(slots < place, padded_after, jnp.where(slots == place, long_doc, padded_before))
    return result.astype(jnp.int32)


def levels(own_key, dims, pieces, low, largest):
    loudness = 1.0
    for dim, parts in pieces:
        heights = jax.random.uniform(jax.random.fold_in(jax.random.fold_in(own_key, 6), dim), (parts,), jnp.float32, low / len(pieces), largest / len(pieces))
        loudness = loudness * jnp.repeat(jnp.exp(heights), dims[dim] // parts).reshape((-1,) + (1,) * (len(dims) - 1 - dim))
    return loudness


def scatter_about(key, extent, deviation, bound, shards=(), held_as=jnp.bfloat16):
    gain = levels(key, extent, shards, -0.22, 0.18) if shards else 1.0
    values = jax.random.normal(key, extent, jnp.float32) * deviation * gain
    return jnp.minimum(jnp.maximum(values, -bound), bound).astype(held_as)


def setup_inputs(seed: int = 0) -> dict:
    seeds = jax.random.split(jax.random.key(seed), 13)
    tokens = scatter_about(seeds[0], (MICRO, ROWS, D), 1.0, 6.0, ((1, 256),))
    lengths = draw_lengths(jax.random.fold_in(seeds[12], 71), 0)
    gain_attn = jnp.clip(1.0 + 0.15 * jax.random.normal(seeds[2], (D,), jnp.float32), 0.25, 1.75).astype(jnp.bfloat16)
    w_query = scatter_about(seeds[3], (D, QD), D ** -0.5, 0.25, ((0, 32), (1, 8)))
    w_key = scatter_about(seeds[4], (D, KVD), D ** -0.5, 0.25, ((0, 32), (1, 8)))
    w_value = scatter_about(seeds[5], (D, KVD), D ** -0.5, 0.25, ((0, 32), (1, 8)))
    w_out = scatter_about(seeds[6], (QD, D), 3 ** -0.5, 3.5, ((0, 32), (1, 8)))
    gain_ffn = jnp.clip(1.0 + 0.15 * jax.random.normal(seeds[7], (D,), jnp.float32), 0.25, 1.75).astype(jnp.bfloat16)
    w_gate = scatter_about(seeds[8], (D, FF), D ** -0.5, 0.25, ((0, 32), (1, 8)))
    w_up = scatter_about(seeds[9], (D, FF), D ** -0.5, 0.25, ((0, 32), (1, 8)))
    w_down = scatter_about(seeds[10], (FF, D), FF ** -0.5, 0.15625, ((0, 32), (1, 8)))
    cotangent = scatter_about(seeds[11], (MICRO, ROWS, D), 1.0, 6.0, ((1, 256),))
    return {"tokens": tokens, "lengths": lengths, "gain_attn": gain_attn, "w_query": w_query, "w_key": w_key, "w_value": w_value, "w_out": w_out, "gain_ffn": gain_ffn, "w_gate": w_gate, "w_up": w_up, "w_down": w_down, "cotangent": cotangent}


@jax.custom_vjp
def low(v):
    return lax.optimization_barrier(v.astype(jnp.bfloat16)).astype(jnp.float32)

@jax.custom_vjp
def low_back(v):
    return v

def low_keep(v):
    return (low(v), None)

def low_pass(kept, grad):
    return (grad,)

def back_keep(v):
    return (v, None)

def back_low(kept, grad):
    return (low(grad),)
low.defvjp(low_keep, low_pass)
low_back.defvjp(back_keep, back_low)
EPSILON = 1e-05
ROPE_BASE = 100000.0
MASKED = -1e+30

def product(first_op, second_op):
    return jnp.dot(first_op, second_op, precision=lax.Precision.HIGHEST, preferred_element_type=jnp.float32)

def rms_scale(values):
    return lax.rsqrt(lax.optimization_barrier(jnp.mean(values * values, axis=-1, keepdims=True)) + EPSILON)

def doc_layout(doc_sizes, places):
    doc_ends = jnp.cumsum(doc_sizes)
    passed = places[:, None] >= doc_ends[None, :]
    segment = lax.optimization_barrier(jnp.sum(passed.astype(jnp.int32), axis=1))
    before = lax.optimization_barrier(jnp.sum(jnp.where(passed, doc_sizes[None, :], 0), axis=1))
    return (segment, places - before)

def rotary(positions):
    half_size = HEAD // 2
    frequencies = ROPE_BASE ** (-jnp.arange(half_size, dtype=jnp.float32) / half_size)
    angles = positions.astype(jnp.float32)[:, None] * frequencies[None, :]
    angles = jnp.concatenate([angles, angles], axis=1)
    return (jnp.cos(angles), jnp.sin(angles))

def turned(values):
    half_size = values.shape[-1] // 2
    return jnp.concatenate([-values[..., half_size:], values[..., :half_size]], axis=-1)

def rotate(values, cosine, sine_table):
    return values * cosine[:, None, :] + turned(values) * sine_table[:, None, :]

def decoder_layer(x_rows, gain_attn, w_query, w_key, w_value, w_out, gain_ffn, w_gate, w_up, w_down, segment, cosine, sine_table):
    row_count = x_rows.shape[0]
    groups = HEADS // KV_HEADS
    normed = low(x_rows * rms_scale(x_rows) * gain_attn)
    queries = low_back(product(normed, w_query)).reshape(row_count, HEADS, HEAD)
    keys_all = low_back(product(normed, w_key)).reshape(row_count, KV_HEADS, HEAD)
    values_all = low(low_back(product(normed, w_value)).reshape(row_count, KV_HEADS, HEAD))
    queries = low(rotate(queries, cosine, sine_table)).reshape(row_count, KV_HEADS, groups, HEAD)
    keys_all = low(rotate(keys_all, cosine, sine_table))
    scores = jnp.einsum('qkgd,skd->kgqs', queries, keys_all, precision=lax.Precision.HIGHEST) * HEAD ** (-0.5)
    scores = low_back(scores)
    places = jnp.arange(row_count)
    allowed = (segment[:, None] == segment[None, :]) & (places[None, :] <= places[:, None])
    scores = jnp.where(allowed, scores, MASKED)
    weights = jnp.exp(scores - lax.optimization_barrier(jnp.max(scores, axis=-1, keepdims=True)))
    probabilities = low(weights / lax.optimization_barrier(jnp.sum(weights, axis=-1, keepdims=True)))
    mixture = jnp.einsum('kgqs,skd->qkgd', probabilities, values_all, precision=lax.Precision.HIGHEST)
    attended = low(low_back(mixture.reshape(row_count, HEADS * HEAD)))
    middle = x_rows + low_back(product(attended, w_out))
    normed_ffn = low(middle * rms_scale(middle) * gain_ffn)
    gate_proj = low_back(product(normed_ffn, w_gate))
    up_proj = low_back(product(normed_ffn, w_up))
    hidden = low(jax.nn.silu(gate_proj) * up_proj)
    return middle + low_back(product(hidden, w_down))

def reference(tokens, lengths, gain_attn, w_query, w_key, w_value, w_out, gain_ffn, w_gate, w_up, w_down, cotangent):
    params = tuple((weight_arg.astype(jnp.float32) for weight_arg in (gain_attn, w_query, w_key, w_value, w_out, gain_ffn, w_gate, w_up, w_down)))
    group_rows = tokens.reshape(MICRO * N_DP, GROUP, D)
    group_back = cotangent.reshape(MICRO * N_DP, GROUP, D)
    group_sizes = lengths.reshape(MICRO * N_DP, NDOC)

    def one_group(totals, group_items):
        rows_in, rows_back, doc_sizes = group_items
        segment, positions = doc_layout(doc_sizes, jnp.arange(GROUP).astype(jnp.int32))
        cosine, sine_table = rotary(positions)

        def forward(x_rows, *weight_list):
            return decoder_layer(x_rows, *weight_list, segment, cosine, sine_table)
        result, pullback = jax.vjp(forward, rows_in.astype(jnp.float32), *params)
        gradients = pullback(rows_back.astype(jnp.float32))
        totals = tuple((left_term + right_term for left_term, right_term in zip(totals, gradients[1:])))
        return (totals, (result.astype(jnp.bfloat16), gradients[0]))
    zeros_init = tuple((jnp.zeros(weight_arg.shape, jnp.float32) for weight_arg in params))
    totals, (outputs, input_grads) = lax.scan(one_group, zeros_init, (group_rows, group_back, group_sizes))
    block_out = outputs.reshape(MICRO, ROWS, D)
    d_tokens = input_grads.reshape(MICRO, ROWS, D)
    return (block_out, d_tokens, totals[0], totals[1], totals[2], totals[3], totals[4], totals[5], totals[6], totals[7], totals[8])
```

```python
import jax
import jax.numpy as jnp
from jax import lax
from jax.experimental import pallas as pl
from jax.experimental.pallas import tpu as pltpu
from jax.sharding import Mesh
from jax.sharding import PartitionSpec as P

HEADS = 9
KV_HEADS = 3
HEAD = 64
D = 576
FF = 1536
GROUP = 1024
STRETCH = 128
LANES = 128
CHUNK = 256
FF_CHUNK = 512
PAD_K = 640
BLOCK_K = 40
EPSILON = 1e-05
ROPE_BASE = 100000.0
MASKED = -1e30
F32 = jnp.float32
BF16 = jnp.bfloat16


def mm(a, b):
    return lax.dot_general(a, b, (((1,), (0,)), ((), ())), preferred_element_type=F32)


def mm_nt(a, b):
    return lax.dot_general(a, b, (((1,), (1,)), ((), ())), preferred_element_type=F32)


def mm_tn(a, b):
    return lax.dot_general(a, b, (((0,), (0,)), ((), ())), preferred_element_type=F32)


def rotate_lanes(values, cosine, sine_low, sine_high):
    parts = []
    for start in range(0, values.shape[1], LANES):
        part = values[:, start : start + LANES]
        parts.append(
            part * cosine
            + pltpu.roll(part, LANES - HEAD // 2, 1) * sine_low
            + pltpu.roll(part, HEAD // 2, 1) * sine_high
        )
    return jnp.concatenate(parts, axis=1)


def unpermute(values, table):
    high = values.astype(BF16)
    low = (values - high.astype(F32)).astype(BF16)
    return mm_nt(high, table) + mm_nt(low, table)


def inverse_rms(values):
    return lax.rsqrt(jnp.mean(values * values, axis=-1, keepdims=True) + EPSILON)


def own_rows(ref):
    return jnp.concatenate([ref[pl.ds(0, STRETCH), :], ref[pl.ds(GROUP, STRETCH), :]], axis=0)


def layer_kernel(
    x_ref,
    back_ref,
    bias_ref,
    cos_ref,
    low_ref,
    high_ref,
    place_a_ref,
    place_b_ref,
    place_bt_ref,
    rows_ref,
    lanes_ref,
    attn_w_ref,
    gate_w_ref,
    up_w_ref,
    down_w_ref,
    core_ref,
    *refs,
):
    out_ref, d_middle_ref, d_normed_ref, d_pairs_ref, w_pairs_ref, gain_ref = refs[:6]
    mine_a, other_a, mine_t, other_t, mine_d, other_d = (
        refs[6 + 4 * i : 10 + 4 * i] for i in range(6)
    )
    (
        attn_w,
        normed,
        keys,
        values,
        probs,
        mixed,
        mixed_low,
        middle_ref,
        hidden_ref,
        d_gate_s,
        d_up_s,
        d_query,
        shared,
        attn_g,
    ) = refs[30:]
    core, x_pos, y_pos = core_ref[0], core_ref[1], core_ref[2]

    def put(first, second, cols, value):
        @pl.when(core == 0)
        def _():
            for k in range(4):
                first[k][:, cols] = value[k * 160 : (k + 1) * 160]

        @pl.when(core == 1)
        def _():
            for k in range(4):
                second[k][:, cols] = value[k * 160 : (k + 1) * 160]

    groups = HEADS // KV_HEADS
    own = 2 * STRETCH
    chunks = 2 * GROUP // CHUNK
    gain_rows = attn_w_ref[:, :LANES]
    row_mask = rows_ref[...].astype(F32)
    gain_attn = jnp.sum(mm(gain_rows, lanes_ref[0]) * row_mask, axis=0, keepdims=True)
    gain_ffn = jnp.sum(mm(gain_rows, lanes_ref[1]) * row_mask, axis=0, keepdims=True)
    gain_ref[...] = gain_attn
    for start in range(0, FF, FF_CHUNK):
        cols = slice(start, start + FF_CHUNK)
        attn_w[:, cols] = mm(place_b_ref[...], attn_w_ref[:, cols]).astype(BF16)
    w_pairs_ref[:, :256] = attn_w[:, 512:768]
    w_pairs_ref[:, 256:] = attn_w[:, 1280:]

    def project(step, carry):
        rows = pl.ds(pl.multiple_of(step * CHUNK, CHUNK), CHUNK)
        x_rows = x_ref[rows, :].astype(F32)
        scaled = (x_rows * inverse_rms(x_rows) * gain_attn).astype(BF16)
        normed[rows, :] = scaled
        turned_keys = rotate_lanes(
            mm(scaled, attn_w[:, 512:768]), cos_ref[rows, :], low_ref[rows, :], high_ref[rows, :]
        )
        keys[rows, :] = turned_keys.astype(BF16)
        values[rows, :] = mm(scaled, attn_w[:, 1280:]).astype(BF16)
        return carry

    lax.fori_loop(0, chunks, project, 0)

    cos_own, low_own, high_own = own_rows(cos_ref), own_rows(low_ref), own_rows(high_ref)
    normed_own = own_rows(normed)
    scale = HEAD ** (-0.5)
    queries = rotate_lanes(mm(normed_own, attn_w[:, :640]), cos_own, low_own, high_own)
    queries = (queries.astype(BF16).astype(F32) * scale).astype(BF16)

    def stacked(array, micro, group):
        rows = slice(micro * STRETCH, (micro + 1) * STRETCH)
        return jnp.concatenate(
            [
                array[rows, HEAD * (group * groups + j) : HEAD * (1 + group * groups + j)]
                for j in range(groups)
            ],
            axis=0,
        )

    for micro in range(2):
        bias = bias_ref[micro]
        bias = jnp.concatenate([bias] * groups, axis=0)
        rows = slice(micro * GROUP, (micro + 1) * GROUP)
        for group in range(KV_HEADS):
            key_rows = keys[rows, HEAD * (group + 1) : HEAD * (group + 2)]
            value_rows = values[rows, HEAD * (group + 1) : HEAD * (group + 2)]
            scores = mm_nt(stacked(queries, micro, group), key_rows) + bias
            weights = jnp.exp(scores - jnp.max(scores, axis=-1, keepdims=True))
            total = jnp.sum(weights, axis=-1, keepdims=True)
            low_probs = (weights * (1.0 / total)).astype(BF16)
            probs[micro * KV_HEADS + group] = low_probs
            mix = mm(low_probs, value_rows)
            mixed[micro * KV_HEADS + group] = mix
            for j in range(groups):
                head = group * groups + j
                mixed_low[
                    micro * STRETCH : (micro + 1) * STRETCH, HEAD * head : HEAD * (head + 1)
                ] = mix[j * STRETCH : (j + 1) * STRETCH].astype(BF16)

    x_own = own_rows(x_ref).astype(F32)
    middle = x_own + mm(mixed_low[...], attn_w[:, 768:1344])
    middle_ref[...] = middle
    scale_ffn = inverse_rms(middle)
    normed_ffn = mm((middle * scale_ffn * gain_ffn).astype(BF16), place_a_ref[...]).astype(BF16)
    back = back_ref[...]
    for start in range(0, FF, FF_CHUNK):
        cols = slice(start, start + FF_CHUNK)
        gate = mm(normed_ffn, gate_w_ref[:, cols])
        up = mm(normed_ffn, up_w_ref[:, cols])
        sig = 1.0 / (1.0 + jnp.exp(-gate))
        silu = gate * sig
        hidden_ref[:, cols] = (silu * up).astype(BF16)
        d_hidden = mm_nt(back, down_w_ref[cols, :])
        d_gate_s[:, cols] = (d_hidden * up * (sig + silu * (1.0 - sig))).astype(BF16)
        d_up_s[:, cols] = (d_hidden * silu).astype(BF16)
    hidden = hidden_ref[...]
    out_ref[...] = (middle + mm(hidden, down_w_ref[...])).astype(BF16)
    d_rows = jnp.zeros((2 * STRETCH, PAD_K), F32)
    for start in range(0, FF, FF_CHUNK):
        cols = slice(start, start + FF_CHUNK)
        d_gate, d_up = d_gate_s[:, cols], d_up_s[:, cols]
        shared[cols, :D] = mm_tn(hidden_ref[:, cols], back)
        put(mine_a, other_a, cols, mm_tn(normed_ffn, d_gate).astype(BF16))
        put(other_a, mine_a, cols, mm_tn(normed_ffn, d_up).astype(BF16))
        d_rows = d_rows + mm_nt(d_gate, gate_w_ref[:, cols]) + mm_nt(d_up, up_w_ref[:, cols])
    d_normed_ffn = unpermute(d_rows, place_a_ref[...])
    middle = middle_ref[...]
    g_gain_ffn = jnp.sum(d_normed_ffn * middle * scale_ffn, axis=0, keepdims=True)
    d_scaled = d_normed_ffn * gain_ffn
    d_middle = (
        back.astype(F32)
        + scale_ffn * d_scaled
        - middle * scale_ffn**3 * jnp.mean(d_scaled * middle, axis=-1, keepdims=True)
    )
    d_middle_ref[...] = d_middle
    d_branch = d_middle.astype(BF16)
    attn_g[:, 768:1344] = mm_tn(mixed_low[...], d_branch).astype(BF16)
    d_mixed = mm_nt(d_branch, attn_w[:, 768:1344]).astype(BF16)

    def split_down(first_part, second_part):
        for k in range(4):
            y_index = lax.rem(y_pos + 4 - k, 4)
            for j in range(4):
                x_index = lax.rem(x_pos + 4 - j, 4)
                for z in range(2):
                    start = (z * 16 + x_index * 4 + y_index) * 48
                    for half, part in enumerate((first_part, second_part)):
                        rows = pl.ds(pl.multiple_of(start + half * 24, 8), 24)
                        part[k][2 * j + z] = shared[rows, :D].astype(BF16)

    @pl.when(core == 0)
    def _():
        split_down(mine_d, other_d)

    @pl.when(core == 1)
    def _():
        split_down(other_d, mine_d)

    d_query[...] = jnp.zeros_like(d_query)
    shared[...] = jnp.zeros_like(shared)
    for micro in range(2):
        rows = slice(micro * GROUP, (micro + 1) * GROUP)
        own_part = slice(micro * STRETCH, (micro + 1) * STRETCH)
        for group in range(KV_HEADS):
            key_rows = keys[rows, HEAD * (group + 1) : HEAD * (group + 2)]
            value_rows = values[rows, HEAD * (group + 1) : HEAD * (group + 2)]
            d_mix = jnp.concatenate(
                [
                    d_mixed[
                        own_part, HEAD * (group * groups + j) : HEAD * (group * groups + j + 1)
                    ]
                    for j in range(groups)
                ],
                axis=0,
            )
            delta = jnp.sum(
                d_mix.astype(F32) * mixed[micro * KV_HEADS + group], axis=-1, keepdims=True
            )
            low_probs = probs[micro * KV_HEADS + group]
            d_probs = mm_nt(d_mix, value_rows)
            d_scores = (low_probs.astype(F32) * (d_probs - delta)).astype(BF16)
            d_rows = mm(d_scores, key_rows) * scale
            for j in range(groups):
                head = group * groups + j
                d_query[own_part, HEAD * head : HEAD * (head + 1)] = d_rows[
                    j * STRETCH : (j + 1) * STRETCH
                ]
            shared[rows, HEAD * (group + 1) : HEAD * (group + 2)] = mm_tn(
                d_scores, stacked(queries, micro, group)
            )
            shared[rows, 256 + HEAD * (group + 1) : 256 + HEAD * (group + 2)] = mm_tn(
                low_probs, d_mix
            )

    d_query_low = rotate_lanes(d_query[...], cos_own, -low_own, -high_own).astype(BF16)
    g_query = mm_tn(normed_own, d_query_low)
    d_normed = mm_nt(d_query_low, attn_w[:, :640])
    d_normed_ref[...] = d_normed
    g_gain_attn = jnp.sum(d_normed * x_own * inverse_rms(x_own), axis=0, keepdims=True)

    def finish(step, carry):
        rows = pl.ds(pl.multiple_of(step * CHUNK, CHUNK), CHUNK)
        key_part = rotate_lanes(
            shared[rows, :256], cos_ref[rows, :], -low_ref[rows, :], -high_ref[rows, :]
        ).astype(BF16)
        value_part = shared[rows, 256:512].astype(BF16)
        d_pairs_ref[rows, :256] = key_part
        d_pairs_ref[rows, 256:] = value_part
        x_rows = x_ref[rows, :].astype(F32)
        d_rows = mm_nt(key_part, attn_w[:, 512:768]) + mm_nt(value_part, attn_w[:, 1280:])
        return carry + jnp.sum(d_rows * x_rows * inverse_rms(x_rows), axis=0, keepdims=True)

    g_gain_attn = lax.fori_loop(0, chunks, finish, g_gain_attn)
    gain_block = mm_nt(row_mask.astype(BF16) * g_gain_attn.astype(BF16), lanes_ref[0])
    gain_block = gain_block + mm_nt(row_mask.astype(BF16) * g_gain_ffn.astype(BF16), lanes_ref[1])
    all_normed = normed[...]
    g_key = mm_tn(all_normed, d_pairs_ref[:, :256])
    g_value = mm_tn(all_normed, d_pairs_ref[:, 256:])
    attn_g[:, :576] = g_query[:, :576].astype(BF16)
    attn_g[:, 576:768] = g_key[:, 64:].astype(BF16)
    attn_g[:, 1344:1536] = g_value[:, 64:].astype(BF16)
    for start in (0, 768):
        part = mm(place_bt_ref[...], attn_g[:, start : start + 768])
        first, second = (mine_t, other_t) if start == 0 else (other_t, mine_t)
        put(first, second, slice(LANES, 768), part[:, LANES:].astype(BF16))
        put(first, second, slice(0, LANES), (part[:, :LANES] + gain_block).astype(BF16))


def assemble_kernel(core_ref, *refs):
    mine_a, other_a, mine_t, other_t, mine_d, other_d = (
        refs[4 * i : 4 + 4 * i] for i in range(6)
    )
    gate_ref, up_ref, attn_ref, down_ref = refs[24:]
    core, x_pos, y_pos = core_ref[0], core_ref[1], core_ref[2]

    def join(gate_part, up_part, query_part, out_part, first_part, second_part):
        for k in range(4):
            rows = slice(k * 160, (k + 1) * 160)
            gate_ref[rows, :] = gate_part[k][...]
            up_ref[rows, :] = up_part[k][...]
            attn_ref[rows, :768] = query_part[k][...]
            attn_ref[rows, 768:] = out_part[k][...]
            y_index = lax.rem(y_pos + 4 - k, 4)
            for j in range(4):
                x_index = lax.rem(x_pos + 4 - j, 4)
                for z in range(2):
                    for half, part in enumerate((first_part, second_part)):
                        down_ref[z * 16 + x_index * 4 + y_index, half] = part[k][2 * j + z]

    @pl.when(core == 0)
    def _():
        join(mine_a, other_a, mine_t, other_t, mine_d, other_d)

    @pl.when(core == 1)
    def _():
        join(other_a, mine_a, other_t, mine_t, other_d, mine_d)


def final_kernel(
    x_ref, gain_ref, w_pairs_ref, d_middle_ref, d_normed_ref, *refs
):
    piece_refs, out_ref = refs[:-1], refs[-1]
    d_pairs = piece_refs[0][...].astype(F32)
    for piece in piece_refs[1:]:
        d_pairs = d_pairs + piece[...].astype(F32)
    d_pairs = d_pairs.astype(BF16)
    x_rows = x_ref[...].astype(F32)
    scale = inverse_rms(x_rows)
    d_scaled = (d_normed_ref[...] + mm_nt(d_pairs, w_pairs_ref[...])) * gain_ref[...]
    out_ref[...] = (
        d_middle_ref[...]
        + scale * d_scaled
        - x_rows * scale**3 * jnp.mean(d_scaled * x_rows, axis=-1, keepdims=True)
    )


def vmem_call(kernel, outs, scratch=(), flops=0, moved=0, specs=None):
    return pl.pallas_call(
        kernel,
        out_shape=outs,
        **({} if specs is None else {"in_specs": specs}),
        scratch_shapes=list(scratch),
        compiler_params=pltpu.CompilerParams(vmem_limit_bytes=60 * 1024 * 1024),
        cost_estimate=pl.CostEstimate(flops=flops, bytes_accessed=moved, transcendentals=0),
    )


def run_layer(x_all, back, tables, places, gain_maps, weights, spot):
    own = 2 * STRETCH
    full = 2 * GROUP
    shape = jax.ShapeDtypeStruct
    outs = (
        shape((own, D), BF16),
        shape((own, D), F32),
        shape((own, D), F32),
        shape((full, 512), BF16),
        shape((D, 512), BF16),
        shape((1, D), F32),
    )
    outs = outs + (shape((160, FF), BF16),) * 8
    outs = outs + (shape((160, 768), BF16),) * 8
    outs = outs + (shape((8, 24, D), BF16),) * 8
    scratch = (
        pltpu.VMEM((D, FF), BF16),
        pltpu.VMEM((full, D), BF16),
        pltpu.VMEM((full, 256), BF16),
        pltpu.VMEM((full, 256), BF16),
        pltpu.VMEM((6, 3 * STRETCH, GROUP), BF16),
        pltpu.VMEM((6, 3 * STRETCH, HEAD), F32),
        pltpu.VMEM((own, D), BF16),
        pltpu.VMEM((own, D), F32),
        pltpu.VMEM((own, FF), BF16),
        pltpu.VMEM((own, FF), BF16),
        pltpu.VMEM((own, FF), BF16),
        pltpu.VMEM((own, PAD_K), F32),
        pltpu.VMEM((full, PAD_K), F32),
        pltpu.VMEM((D, FF), BF16),
    )
    specs = [pl.BlockSpec(memory_space=pltpu.VMEM)] * 15
    specs.append(pl.BlockSpec(memory_space=pltpu.SMEM))
    return vmem_call(layer_kernel, outs, scratch, 15 * 10**9, 60 * 10**6, specs)(
        x_all, back, *tables, *places, *gain_maps, *weights, spot
    )


def run_assemble(spot, pieces):
    shape = jax.ShapeDtypeStruct
    outs = (
        shape((PAD_K, FF), BF16),
        shape((PAD_K, FF), BF16),
        shape((PAD_K, FF), BF16),
        shape((32, 2, 24, D), BF16),
    )
    specs = [pl.BlockSpec(memory_space=pltpu.SMEM)]
    specs = specs + [pl.BlockSpec(memory_space=pltpu.VMEM)] * 24
    gate, up, attn, down = vmem_call(assemble_kernel, outs, (), 0, 14 * 10**6, specs)(
        spot, *pieces
    )
    return attn, gate, up, down.reshape(FF, D)


def run_final(x_own, gain, w_pairs, d_middle, d_normed, pieces):
    outs = jax.ShapeDtypeStruct((2 * STRETCH, D), F32)
    return vmem_call(final_kernel, outs, (), 3 * 10**8, 4 * 10**6)(
        x_own, gain, w_pairs, d_middle, d_normed, *pieces
    )


def row_tables(doc_sizes, key_places, query_places):
    ends = jnp.cumsum(doc_sizes)

    def start_of(places):
        passed = places[:, None] >= ends[None, :]
        return jnp.sum(jnp.where(passed, doc_sizes[None, :], 0), axis=1)

    starts = start_of(query_places)
    allowed = (key_places[None, :] >= starts[:, None]) & (
        key_places[None, :] <= query_places[:, None]
    )
    bias = jnp.where(allowed, 0.0, MASKED).astype(F32)
    positions = key_places - start_of(key_places)
    half = HEAD // 2
    frequencies = ROPE_BASE ** (-jnp.arange(half, dtype=F32) / half)
    angles = positions.astype(F32)[:, None] * frequencies[None, :]
    return bias, jnp.cos(angles), jnp.sin(angles)


def rotary_tables(cosine, sine):
    zero = jnp.zeros_like(sine)
    return (
        jnp.concatenate([cosine] * 4, axis=1),
        jnp.concatenate([-sine, zero] * 2, axis=1),
        jnp.concatenate([zero, sine] * 2, axis=1),
    )


def ring(values, axis, step, size=4):
    return lax.ppermute(values, axis, [(i, (i + step) % size) for i in range(size)])


def swap(values):
    return lax.ppermute(values, "c", [(0, 1), (1, 0)])


def ring_z(values, step):
    def index(z):
        return (z % 2) * 4 + z // 2

    pairs = [(index(z), index((z + step) % 8)) for z in range(8)]
    return lax.ppermute(values, ("zl", "zh"), pairs)


def rolled(stack, start):
    return lax.dynamic_slice_in_dim(jnp.concatenate([stack, stack], axis=0), start, stack.shape[0], 0)


def gather_weights(shards, spot):
    w_query, w_key, w_value, w_out, w_gate, w_up, w_down, gain_attn, gain_ffn = shards
    first = spot["core"] == 0

    def halves(a_part, left, right, down):
        gains = jnp.concatenate([gain_attn, gain_ffn, jnp.zeros((252,), BF16)])[None]
        rows = jnp.concatenate([a_part, left, right], axis=1)
        rows = jnp.concatenate([rows, gains, jnp.zeros((5, 288), BF16)], axis=0)
        return jnp.concatenate([rows, down], axis=1)

    lower = halves(w_gate, w_query, w_key, w_down[:24])
    upper = halves(w_up, w_out, w_value, w_down[24:])
    keep = jnp.where(first, lower, upper)
    taken = swap(jnp.where(first, upper, lower))
    pair = jnp.concatenate(
        [jnp.where(first, keep, taken), jnp.where(first, taken, keep)], axis=1
    )
    column = [pair] + [ring_z(pair, k) for k in range(1, 8)]
    stack = jnp.stack([column[0]] + column[:0:-1])
    stack = rolled(stack, lax.rem(8 - spot["z"], 8)).reshape(4, 2, 24, 2, 360)

    def wide(part, rows):
        return jnp.transpose(part, (1, 2, 0, 3, 4)).reshape(rows, -1)

    a_block = jnp.pad(wide(stack[:, :, :18, :, :192], 36), ((0, 4), (0, 0)))
    t_block = jnp.concatenate(
        [wide(stack[:, :, :18, :, 192:264], 36), wide(stack[:, :, :18, :, 264:288], 36)], axis=1
    )
    gain_rows = jnp.pad(stack[0, :, 18, 0, :36], ((0, 2), (0, 768 - 36)))
    t_block = jnp.concatenate([t_block, gain_rows], axis=0)
    d_block = wide(stack[..., 288:], 48).reshape(2, 24, D)

    def along(block, axis):
        return [block] + [ring(block, axis, k) for k in range(1, 4)]

    a_block = jnp.concatenate(along(a_block, "y"), axis=0)
    t_block = jnp.concatenate(along(t_block, "x"), axis=0)
    d_block = jnp.concatenate(along(d_block, "x"), axis=0)
    mine_a, mine_t, mine_d = along(a_block, "x"), along(t_block, "y"), along(d_block, "y")
    other_a, other_t, other_d = ([swap(p) for p in part] for part in (mine_a, mine_t, mine_d))
    return (*mine_a, *other_a, *mine_t, *other_t, *mine_d, *other_d)


def total(parts):
    result = parts[0].astype(F32)
    for part in parts[1:]:
        result = result + part.astype(F32)
    return result


def scatter_along(chunks, axis):
    return [chunks[0]] + [ring(chunks[k], axis, 4 - k) for k in range(1, 4)]


def rows_of(parts, start, size):
    return total([part[start : start + size] for part in parts]).astype(BF16)


def reduce_grads(pieces, spot):
    first = spot["core"] == 0
    mine_a, other_a, mine_t, other_t, mine_d, other_d = (
        pieces[4 * i : 4 * i + 4] for i in range(6)
    )

    def paired(mine, other):
        return [total([m, swap(o)]).astype(BF16) for m, o in zip(mine, other)]

    def stage(mine, other, axis, size):
        received = scatter_along(paired(mine, other), axis)
        return [rows_of(received, k * size, size) for k in range(4)]

    a_parts = stage(mine_a, other_a, "x", 40)
    t_parts = stage(mine_t, other_t, "y", 40)
    d_parts = stage(mine_d, other_d, "y", 2)
    a_block = total(scatter_along(a_parts, "y")).astype(BF16)
    t_block = total(scatter_along(t_parts, "x")).astype(BF16)
    d_block = total(scatter_along(d_parts, "x")).astype(BF16)

    def narrow(part, rows, width):
        return jnp.transpose(part.reshape(2, rows, 4, 2, width), (2, 0, 1, 3, 4))

    rows = jnp.concatenate(
        [
            narrow(a_block[:36], 18, 192),
            narrow(t_block[:36, :D], 18, 72),
            narrow(t_block[:36, D:], 18, 24),
        ],
        axis=-1,
    )
    gain_rows = jnp.broadcast_to(t_block[36:38, :36][None, :, None, None], (4, 2, 1, 2, 36))
    gain_rows = jnp.pad(gain_rows, ((0, 0), (0, 0), (0, 5), (0, 0), (0, 252)))
    packets = jnp.concatenate(
        [jnp.concatenate([rows, gain_rows], axis=2), narrow(d_block, 24, 72)], axis=-1
    )
    packets = rolled(packets.reshape(8, 24, 720), spot["z"])
    received = [packets[0]] + [ring_z(packets[k], k) for k in range(1, 8)]
    summed = total(received)
    gain_stack = jnp.stack([part[18, :36] for part in [received[0]] + received[:0:-1]])
    gains = jnp.sum(rolled(gain_stack, lax.rem(8 - spot["z"], 8)).astype(F32), axis=0)
    low_half, high_half = summed[:, :360], summed[:, 360:]
    keep = jnp.where(first, low_half, high_half)
    taken = swap(jnp.where(first, high_half, low_half).astype(BF16)).astype(F32)
    lower = jnp.where(first, keep, taken)
    upper = jnp.where(first, taken, keep)
    return (
        gains[:18],
        lower[:18, 192:264],
        lower[:18, 264:288],
        upper[:18, 264:288],
        upper[:18, 192:264],
        gains[18:],
        lower[:18, :192],
        upper[:18, :192],
        jnp.concatenate([lower[:, 288:], upper[:, 288:]], axis=0),
    )


def body(
    tokens,
    lengths,
    gain_attn,
    w_query,
    w_key,
    w_value,
    w_out,
    gain_ffn,
    w_gate,
    w_up,
    w_down,
    cotangent,
):
    core, z_high, z_low = lax.axis_index("c"), lax.axis_index("zh"), lax.axis_index("zl")
    x_pos, y_pos = lax.axis_index("x"), lax.axis_index("y")
    spot = {"core": core, "z": z_high * 2 + z_low}
    spot_array = jnp.stack([core, x_pos, y_pos]).astype(jnp.int32)
    shards = (w_query, w_key, w_value, w_out, w_gate, w_up, w_down, gain_attn, gain_ffn)
    pieces = gather_weights(shards, spot)

    x_own = tokens.reshape(2 * STRETCH, D)
    x_mine = [x_own] + [ring(x_own, "zh", k) for k in range(1, 4)]
    x_parts = x_mine + [swap(part) for part in x_mine]
    x_all = jnp.concatenate(
        [part[m * STRETCH : (m + 1) * STRETCH] for m in range(2) for part in x_parts], axis=0
    )
    slot = jnp.arange(8, dtype=jnp.int32)
    holder = lax.rem(z_high + 4 - lax.rem(slot, 4), 4) * 2 + jnp.where(slot < 4, core, 1 - core)
    steps = jnp.arange(STRETCH, dtype=jnp.int32)
    key_places = (holder[:, None] * STRETCH + steps[None, :]).reshape(GROUP)
    query_places = (z_high * 2 + core) * STRETCH + steps
    made = [row_tables(lengths[m, 0], key_places, query_places) for m in range(2)]
    bias = jnp.stack([made[0][0], made[1][0]])
    tables = (bias,) + rotary_tables(
        jnp.concatenate([made[0][1], made[1][1]]), jnp.concatenate([made[0][2], made[1][2]])
    )
    places, gain_maps = placements(x_pos, y_pos)
    weights = run_assemble(spot_array, pieces)
    results = run_layer(
        x_all, cotangent.reshape(2 * STRETCH, D), tables, places, gain_maps, weights, spot_array
    )
    block_out, d_middle, d_normed, d_pairs, w_pairs, gain = results[:6]

    by_slot = d_pairs.reshape(2, 8, STRETCH, 512)
    other = swap(by_slot[:, 4:])
    joined = (by_slot[:, :4].astype(F32) + other.astype(F32)).astype(BF16)
    sent = [joined[:, k].reshape(2 * STRETCH, 512) for k in range(4)]
    pair_parts = scatter_along(sent, "zh")
    d_tokens = run_final(x_own, gain, w_pairs, d_middle, d_normed, pair_parts)
    grads = reduce_grads(results[6:], spot)
    return (
        block_out.reshape(2, STRETCH, D),
        d_tokens.reshape(2, STRETCH, D),
        *grads,
    )


def placements(x_pos, y_pos):
    feature = jnp.arange(D, dtype=jnp.int32)
    z, x, y, i = feature // 288, (feature // 72) % 4, (feature // 18) % 4, feature % 18
    x_rel, y_rel = lax.rem(x_pos + 4 - x, 4), lax.rem(y_pos + 4 - y, 4)
    start_a, start_b = (x_rel * 4 + y_rel) * BLOCK_K, (y_rel * 4 + x_rel) * BLOCK_K
    inside = z * 18 + i
    columns = jnp.arange(PAD_K, dtype=jnp.int32)
    place_a = ((start_a + inside)[:, None] == columns[None, :]).astype(BF16)
    place_b = ((start_b + inside)[:, None] == columns[None, :]).astype(BF16)
    place_bt = ((start_b + inside)[None, :] == columns[:, None]).astype(BF16)
    row_mask = ((start_b + 36 + z)[None, :] == columns[:, None]).astype(BF16)
    lanes = jnp.arange(LANES, dtype=jnp.int32)[:, None]
    lane_maps = jnp.stack([lanes == i[None, :], lanes == (i + 18)[None, :]]).astype(BF16)
    return (place_a, place_b, place_bt), (row_mask, lane_maps)


def solution(mesh):
    split = Mesh(mesh.devices.reshape(2, 4, 4, 4, 2), ("zl", "x", "y", "zh", "c"))
    rows, columns = ("zl", "x", "y"), ("zh", "c")
    everywhere = P(None, rows + columns, None)
    matrix, vector = P(rows, columns), P(rows)
    in_specs = (
        everywhere,
        P(None, rows, None),
        vector,
        matrix,
        matrix,
        matrix,
        matrix,
        vector,
        matrix,
        matrix,
        matrix,
        everywhere,
    )
    out_specs = (
        everywhere,
        everywhere,
        vector,
        matrix,
        matrix,
        matrix,
        matrix,
        vector,
        matrix,
        matrix,
        matrix,
    )
    return jax.shard_map(body, mesh=split, in_specs=in_specs, out_specs=out_specs, check_vma=False)
```

```python
import jax
import jax.numpy as jnp
from jax import lax
from jax.experimental import pallas as pl
from jax.experimental.pallas import tpu as pltpu
from jax.sharding import Mesh
from jax.sharding import PartitionSpec as P

HEADS = 9
KV_HEADS = 3
HEAD = 64
D = 576
FF = 1536
GROUP = 1024
STRETCH = 128
LANES = 128
CHUNK = 256
FF_CHUNK = 512
PAD_K = 640
BLOCK_K = 40
EPSILON = 1e-05
ROPE_BASE = 100000.0
MASKED = -1e30
F32 = jnp.float32
BF16 = jnp.bfloat16


def mm(a, b):
    return lax.dot_general(a, b, (((1,), (0,)), ((), ())), preferred_element_type=F32)


def mm_nt(a, b):
    return lax.dot_general(a, b, (((1,), (1,)), ((), ())), preferred_element_type=F32)


def mm_tn(a, b):
    return lax.dot_general(a, b, (((0,), (0,)), ((), ())), preferred_element_type=F32)


def rotate_lanes(values, cosine, sine):
    parts = []
    lanes = lax.broadcasted_iota(jnp.int32, (values.shape[0], LANES), 1)
    early = lanes % HEAD < HEAD // 2
    for start in range(0, values.shape[1], LANES):
        part = values[:, start : start + LANES]
        parts.append(
            part * cosine
            + jnp.where(
                early,
                pltpu.roll(part, LANES - HEAD // 2, 1),
                pltpu.roll(part, HEAD // 2, 1),
            )
            * sine
        )
    return jnp.concatenate(parts, axis=1)


def unpermute(values, table):
    high = values.astype(BF16)
    low = (values - high.astype(F32)).astype(BF16)
    return mm_nt(high, table) + mm_nt(low, table)


def inverse_rms(values):
    return lax.rsqrt(jnp.mean(values * values, axis=-1, keepdims=True) + EPSILON)


def layer_kernel(
    spot_ref,
    x_ref,
    back_ref,
    bias_ref,
    cos_ref,
    sine_ref,
    place_a_ref,
    place_b_ref,
    place_bt_ref,
    rows_ref,
    lanes_ref,
    *refs,
):
    mine_a, other_a, mine_b, other_b = (refs[4 * i : 4 * i + 4] for i in range(4))
    out_ref, d_middle_ref, d_normed_ref, d_pairs_ref, w_pairs_ref, gain_ref = refs[16:22]
    g_mine_a, g_other_a, g_mine_b, g_other_b = refs[22:26], refs[26], refs[27:31], refs[31]
    (
        attn_w_ref,
        gate_w_ref,
        up_w_ref,
        down_w_ref,
        attn_w,
        normed,
        keys,
        values,
        probs,
        mixed,
        mixed_low,
        hidden_ref,
        d_gate_s,
        d_up_s,
        d_query,
        shared,
        sems,
    ) = refs[32:]
    attn_g, middle_ref = attn_w_ref, d_middle_ref
    core, x_pos, y_pos, ctx_pos = spot_ref[0], spot_ref[1], spot_ref[2], spot_ref[3]

    def fetch(query_part, out_part, gate_part, up_part):
        for k in range(4):
            rows = pl.ds(k * 160, 160)
            top = pl.ds(0, 160)
            pltpu.make_async_copy(
                query_part[k].at[top], attn_w_ref.at[rows, pl.ds(0, 768)], sems.at[0]
            ).start()
            pltpu.make_async_copy(
                out_part[k].at[top], attn_w_ref.at[rows, pl.ds(768, 768)], sems.at[0]
            ).start()
        for k in range(4):
            rows = pl.ds(k * 160, 160)
            pltpu.make_async_copy(gate_part[k], gate_w_ref.at[rows], sems.at[1]).start()
            pltpu.make_async_copy(up_part[k], up_w_ref.at[rows], sems.at[2]).start()

    @pl.when(core == 0)
    def _():
        fetch(mine_b, other_b, mine_a, other_a)

    @pl.when(core == 1)
    def _():
        fetch(other_b, mine_b, other_a, mine_a)

    def down_start(k, j, half):
        y_index, x_index = lax.rem(y_pos + 4 - k, 4), lax.rem(x_pos + 4 - j, 4)
        return pl.multiple_of((half * 16 + x_index * 4 + y_index) * 48, 16)

    for k in range(4):
        for j in range(4):
            source = pl.ds(160 + 48 * j, 48)
            pltpu.make_async_copy(
                mine_b[k].at[source], down_w_ref.at[pl.ds(down_start(k, j, core), 48)], sems.at[3]
            ).start()
            pltpu.make_async_copy(
                other_b[k].at[source],
                down_w_ref.at[pl.ds(down_start(k, j, 1 - core), 48)],
                sems.at[3],
            ).start()

    def put(owner, value, store_mine, store_other):
        @pl.when(core == owner)
        def _():
            for k in range(4):
                store_mine(k, value[k * 160 : (k + 1) * 160])

        @pl.when(core != owner)
        def _():
            for k in range(4):
                store_other(k, value[k * 160 : (k + 1) * 160])

    def put_a(owner, cols, value):
        def store_mine(k, part):
            g_mine_a[k][:, cols] = part

        def store_other(k, part):
            g_other_a[k * 160 : (k + 1) * 160, cols] = part

        put(owner, value, store_mine, store_other)

    def put_b(owner, cols, value):
        def store_mine(k, part):
            g_mine_b[k][:160, cols] = part

        def store_other(k, part):
            g_other_b[k * 352 : k * 352 + 160, cols] = part

        put(owner, value, store_mine, store_other)

    pltpu.make_async_copy(attn_w_ref, attn_w_ref, sems.at[0]).wait()
    groups = HEADS // KV_HEADS
    own = 2 * STRETCH
    chunks = 2 * GROUP // CHUNK
    gain_rows = attn_w_ref[:, :LANES]
    row_mask = rows_ref[...].astype(F32)
    gain_attn = jnp.sum(mm_nt(gain_rows, lanes_ref[0]) * row_mask, axis=0, keepdims=True)
    gain_ffn = jnp.sum(mm_nt(gain_rows, lanes_ref[1]) * row_mask, axis=0, keepdims=True)
    gain_column = jnp.sum(
        mm_tn(rows_ref[...], gain_rows) * lanes_ref[0].astype(F32), axis=1, keepdims=True
    )
    gain_ref[...] = gain_attn
    for start in range(0, FF, FF_CHUNK):
        cols = slice(start, start + FF_CHUNK)
        attn_w[:, cols] = mm(place_b_ref[...], attn_w_ref[:, cols]).astype(BF16)
    w_pairs_ref[:, :256] = attn_w[:, 512:768]
    w_pairs_ref[:, 256:] = attn_w[:, 1280:]

    def project(step, carry):
        rows = pl.ds(pl.multiple_of(step * CHUNK, CHUNK), CHUNK)
        x_rows = x_ref[rows, :].astype(F32)
        scaled = (x_rows * inverse_rms(x_rows) * gain_attn).astype(BF16)
        normed[rows, :] = scaled
        turned_keys = rotate_lanes(
            mm(scaled, attn_w[:, 512:768]), cos_ref[rows, :], sine_ref[rows, :]
        )
        keys[rows, :] = turned_keys.astype(BF16)
        values[rows, :] = mm(scaled, attn_w[:, 1280:]).astype(BF16)
        return carry

    lax.fori_loop(0, chunks, project, 0)

    own_slot = pl.ds(pl.multiple_of(ctx_pos * own, own), own)
    cos_own, sine_own = cos_ref[own_slot, :], sine_ref[own_slot, :]
    normed_own = normed[own_slot, :]
    scale = HEAD ** (-0.5)
    queries = rotate_lanes(mm(normed_own, attn_w[:, :640]), cos_own, sine_own)
    queries = (queries.astype(BF16).astype(F32) * scale).astype(BF16)

    def of_micro(ref, micro, group):
        lanes = slice(HEAD * (group + 1), HEAD * (group + 2))
        start = micro * STRETCH
        return jnp.concatenate(
            [ref[k * own + start : k * own + start + STRETCH, lanes] for k in range(8)], axis=0
        )

    def stacked(array, micro, group):
        rows = slice(micro * STRETCH, (micro + 1) * STRETCH)
        return jnp.concatenate(
            [
                array[rows, HEAD * (group * groups + j) : HEAD * (1 + group * groups + j)]
                for j in range(groups)
            ],
            axis=0,
        )

    for micro in range(2):
        bias = bias_ref[micro]
        bias = jnp.concatenate([bias] * groups, axis=0)
        for group in range(KV_HEADS):
            key_rows = of_micro(keys, micro, group)
            value_rows = of_micro(values, micro, group)
            scores = mm_nt(stacked(queries, micro, group), key_rows) + bias
            weights = jnp.exp(scores - jnp.max(scores, axis=-1, keepdims=True))
            total = jnp.sum(weights, axis=-1, keepdims=True)
            low_probs = (weights * (1.0 / total)).astype(BF16)
            probs[micro * KV_HEADS + group] = low_probs
            mix = mm(low_probs, value_rows)
            mixed[micro * KV_HEADS + group] = mix
            for j in range(groups):
                head = group * groups + j
                mixed_low[
                    micro * STRETCH : (micro + 1) * STRETCH, HEAD * head : HEAD * (head + 1)
                ] = mix[j * STRETCH : (j + 1) * STRETCH].astype(BF16)

    x_own = x_ref[own_slot, :].astype(F32)
    middle = x_own + mm(mixed_low[...], attn_w[:, 768:1344])
    middle_ref[...] = middle
    scale_ffn = inverse_rms(middle)
    normed_ffn = mm((middle * scale_ffn * gain_ffn).astype(BF16), place_a_ref[...]).astype(BF16)
    back = back_ref[...]
    pltpu.make_async_copy(gate_w_ref, gate_w_ref, sems.at[1]).wait()
    pltpu.make_async_copy(up_w_ref, up_w_ref, sems.at[2]).wait()
    pltpu.make_async_copy(down_w_ref, down_w_ref, sems.at[3]).wait()
    for start in range(0, FF, FF_CHUNK):
        cols = slice(start, start + FF_CHUNK)
        gate = mm(normed_ffn, gate_w_ref[:, cols])
        up = mm(normed_ffn, up_w_ref[:, cols])
        sig = 1.0 / (1.0 + jnp.exp(-gate))
        silu = gate * sig
        hidden_ref[:, cols] = (silu * up).astype(BF16)
        d_hidden = mm_nt(back, down_w_ref[cols, :D])
        d_gate_s[:, cols] = (d_hidden * up * (sig + silu * (1.0 - sig))).astype(BF16)
        d_up_s[:, cols] = (d_hidden * silu).astype(BF16)
    hidden = hidden_ref[...]
    out_ref[...] = (middle + mm(hidden, down_w_ref[:, :D])).astype(BF16)
    d_rows = jnp.zeros((2 * STRETCH, PAD_K), F32)
    for start in range(0, FF, FF_CHUNK):
        cols = slice(start, start + FF_CHUNK)
        d_gate, d_up = d_gate_s[:, cols], d_up_s[:, cols]
        shared[cols, :D] = mm_tn(hidden_ref[:, cols], back)
        put_a(0, cols, mm_tn(normed_ffn, d_gate).astype(BF16))
        put_a(1, cols, mm_tn(normed_ffn, d_up).astype(BF16))
        d_rows = d_rows + mm_nt(d_gate, gate_w_ref[:, cols]) + mm_nt(d_up, up_w_ref[:, cols])
    d_normed_ffn = unpermute(d_rows, place_a_ref[...])
    middle = middle_ref[...]
    g_gain_ffn = jnp.sum(d_normed_ffn * middle * scale_ffn, axis=0, keepdims=True)
    d_scaled = d_normed_ffn * gain_ffn
    d_middle = (
        back.astype(F32)
        + scale_ffn * d_scaled
        - middle * scale_ffn**3 * jnp.mean(d_scaled * middle, axis=-1, keepdims=True)
    )
    d_middle_ref[...] = d_middle
    d_branch = d_middle.astype(BF16)
    attn_g[:D, 768:1344] = mm_tn(mixed_low[...], d_branch).astype(BF16)
    d_mixed = mm_nt(d_branch, attn_w[:, 768:1344]).astype(BF16)

    for k in range(4):
        for j in range(4):
            start = 160 + 48 * j
            g_mine_b[k][start : start + 48, :D] = shared[
                pl.ds(down_start(k, j, core), 48), :D
            ].astype(BF16)
            g_other_b[k * 352 + start : k * 352 + start + 48, :D] = shared[
                pl.ds(down_start(k, j, 1 - core), 48), :D
            ].astype(BF16)
        g_mine_b[k][160:, D:] = jnp.zeros((192, 768 - D), BF16)
        g_other_b[k * 352 + 160 : (k + 1) * 352, D:] = jnp.zeros((192, 768 - D), BF16)

    d_query[...] = jnp.zeros_like(d_query)
    shared[...] = jnp.zeros_like(shared)
    for micro in range(2):
        own_part = slice(micro * STRETCH, (micro + 1) * STRETCH)
        for group in range(KV_HEADS):
            key_rows = of_micro(keys, micro, group)
            value_rows = of_micro(values, micro, group)
            d_mix = jnp.concatenate(
                [
                    d_mixed[
                        own_part, HEAD * (group * groups + j) : HEAD * (group * groups + j + 1)
                    ]
                    for j in range(groups)
                ],
                axis=0,
            )
            delta = jnp.sum(
                d_mix.astype(F32) * mixed[micro * KV_HEADS + group], axis=-1, keepdims=True
            )
            low_probs = probs[micro * KV_HEADS + group]
            d_probs = mm_nt(d_mix, value_rows)
            d_scores = (low_probs.astype(F32) * (d_probs - delta)).astype(BF16)
            d_rows = mm(d_scores, key_rows) * scale
            for j in range(groups):
                head = group * groups + j
                d_query[own_part, HEAD * head : HEAD * (head + 1)] = d_rows[
                    j * STRETCH : (j + 1) * STRETCH
                ]
            d_key_rows = mm_tn(d_scores, stacked(queries, micro, group))
            d_value_rows = mm_tn(low_probs, d_mix)
            left, right = HEAD * (group + 1), 256 + HEAD * (group + 1)
            for k in range(8):
                rows = slice(k * own + micro * STRETCH, k * own + (micro + 1) * STRETCH)
                part = slice(k * STRETCH, (k + 1) * STRETCH)
                shared[rows, left : left + HEAD] = d_key_rows[part]
                shared[rows, right : right + HEAD] = d_value_rows[part]

    d_query_low = rotate_lanes(d_query[...], cos_own, -sine_own).astype(BF16)
    g_query = mm_tn(normed_own, d_query_low)
    d_normed = mm_nt(d_query_low, attn_w[:, :640])
    d_normed_ref[...] = d_normed

    def finish(step, carry):
        rows = pl.ds(pl.multiple_of(step * CHUNK, CHUNK), CHUNK)
        key_part = rotate_lanes(
            shared[rows, :256], cos_ref[rows, :], -sine_ref[rows, :]
        ).astype(BF16)
        value_part = shared[rows, 256:512].astype(BF16)
        d_pairs_ref[rows, :256] = key_part
        d_pairs_ref[rows, 256:] = value_part
        return carry

    lax.fori_loop(0, chunks, finish, 0)
    all_normed = normed[...]
    g_key = mm_tn(all_normed, d_pairs_ref[:, :256])
    g_value = mm_tn(all_normed, d_pairs_ref[:, 256:])
    attn_g[:D, :576] = g_query[:, :576].astype(BF16)
    attn_g[:D, 576:768] = g_key[:, 64:].astype(BF16)
    attn_g[:D, 1344:1536] = g_value[:, 64:].astype(BF16)
    g_gain_attn = (
        jnp.sum(attn_w[:, :640].astype(F32) * g_query, axis=1, keepdims=True)
        + jnp.sum(attn_w[:, 512:768].astype(F32) * g_key, axis=1, keepdims=True)
        + jnp.sum(attn_w[:, 1280:].astype(F32) * g_value, axis=1, keepdims=True)
    ) / gain_column
    gain_block = mm(rows_ref[...], (g_gain_attn * lanes_ref[0].astype(F32)).astype(BF16)) + mm(
        (row_mask * g_gain_ffn).astype(BF16), lanes_ref[1]
    )
    for start in (0, 768):
        part = mm(place_bt_ref[...], attn_g[:D, start : start + 768])
        put_b(start // 768, slice(LANES, 768), part[:, LANES:].astype(BF16))
        put_b(start // 768, slice(0, LANES), (part[:, :LANES] + gain_block).astype(BF16))


def pair_kernel(mine_0, mine_1, mine_2, mine_3, other_ref, *outs):
    size = mine_0.shape[0]
    for k, mine in enumerate((mine_0, mine_1, mine_2, mine_3)):
        other = other_ref[k * size : (k + 1) * size, :]
        outs[k][...] = (mine[...].astype(F32) + other.astype(F32)).astype(BF16)


def stage_kernel(*refs):
    result = total([ref[...] for ref in refs[:4]])
    for k, out in enumerate(refs[4:]):
        part = result[k * BLOCK_K : (k + 1) * BLOCK_K]
        if out.shape[0] > BLOCK_K:
            part = jnp.concatenate([part, result[160 + 48 * k : 208 + 48 * k]], axis=0)
        out[...] = part.astype(BF16)


def total(parts):
    result = parts[0].astype(F32)
    for part in parts[1:]:
        result = result + part.astype(F32)
    return result


def final_kernel(x_ref, gain_ref, w_pairs_ref, d_middle_ref, d_normed_ref, d_pairs_ref, out_ref):
    x_rows = x_ref[...].astype(F32)
    scale = inverse_rms(x_rows)
    d_scaled = (d_normed_ref[...] + mm_nt(d_pairs_ref[...], w_pairs_ref[...])) * gain_ref[...]
    out_ref[...] = (
        d_middle_ref[...]
        + scale * d_scaled
        - x_rows * scale**3 * jnp.mean(d_scaled * x_rows, axis=-1, keepdims=True)
    )


def vmem_call(kernel, outs, scratch=(), flops=0, moved=0, specs=None):
    return pl.pallas_call(
        kernel,
        out_shape=outs,
        **({} if specs is None else {"in_specs": specs}),
        scratch_shapes=list(scratch),
        compiler_params=pltpu.CompilerParams(vmem_limit_bytes=62 * 1024 * 1024),
        cost_estimate=pl.CostEstimate(flops=flops, bytes_accessed=moved, transcendentals=0),
    )


def run_layer(spot, x_all, back, tables, places, gain_maps, pieces):
    own = 2 * STRETCH
    full = 2 * GROUP
    shape = jax.ShapeDtypeStruct
    outs = (
        shape((own, D), BF16),
        shape((own, D), F32),
        shape((own, D), F32),
        shape((full, 512), BF16),
        shape((D, 512), BF16),
        shape((1, D), F32),
    )
    outs = outs + (shape((160, FF), BF16),) * 4 + (shape((640, FF), BF16),)
    outs = outs + (shape((352, 768), BF16),) * 4 + (shape((1408, 768), BF16),)
    scratch = (
        pltpu.VMEM((PAD_K, FF), BF16),
        pltpu.VMEM((PAD_K, FF), BF16),
        pltpu.VMEM((PAD_K, FF), BF16),
        pltpu.VMEM((FF, 768), BF16),
        pltpu.VMEM((D, FF), BF16),
        pltpu.VMEM((full, D), BF16),
        pltpu.VMEM((full, 256), BF16),
        pltpu.VMEM((full, 256), BF16),
        pltpu.VMEM((6, 3 * STRETCH, GROUP), BF16),
        pltpu.VMEM((6, 3 * STRETCH, HEAD), F32),
        pltpu.VMEM((own, D), BF16),
        pltpu.VMEM((own, FF), BF16),
        pltpu.VMEM((own, FF), BF16),
        pltpu.VMEM((own, FF), BF16),
        pltpu.VMEM((own, PAD_K), F32),
        pltpu.VMEM((full, PAD_K), F32),
        pltpu.SemaphoreType.DMA((4,)),
    )
    specs = [pl.BlockSpec(memory_space=pltpu.SMEM)]
    specs = specs + [pl.BlockSpec(memory_space=pltpu.VMEM)] * 10
    specs = specs + [pl.BlockSpec(memory_space=pl.ANY)] * 16
    return vmem_call(layer_kernel, outs, scratch, 15 * 10**9, 60 * 10**6, specs)(
        spot, x_all, back, *tables, *places, *gain_maps, *pieces
    )


def run_pair(mine, other):
    outs = tuple(jax.ShapeDtypeStruct(part.shape, BF16) for part in mine)
    return vmem_call(pair_kernel, outs, (), 10**6, 6 * 10**6)(*mine, other)


def run_stage(parts):
    rows = parts[0].shape[0] // 4
    outs = (jax.ShapeDtypeStruct((rows, parts[0].shape[1]), BF16),) * 4
    return vmem_call(stage_kernel, outs, (), 10**6, 3 * 10**6)(*parts)


def run_final(*args):
    outs = jax.ShapeDtypeStruct((2 * STRETCH, D), F32)
    return vmem_call(final_kernel, outs, (), 3 * 10**8, 4 * 10**6)(*args)


def row_tables(doc_sizes, key_places, query_places):
    ends = jnp.cumsum(doc_sizes)

    def start_of(places):
        passed = places[:, None] >= ends[None, :]
        return jnp.sum(jnp.where(passed, doc_sizes[None, :], 0), axis=1)

    starts = start_of(query_places)
    allowed = (key_places[None, :] >= starts[:, None]) & (
        key_places[None, :] <= query_places[:, None]
    )
    bias = jnp.where(allowed, 0.0, MASKED).astype(F32)
    positions = key_places - start_of(key_places)
    half = HEAD // 2
    frequencies = ROPE_BASE ** (-jnp.arange(half, dtype=F32) / half)
    angles = positions.astype(F32)[:, None] * frequencies[None, :]
    return bias, jnp.cos(angles), jnp.sin(angles)


def rotary_tables(cosine, sine):
    return (
        jnp.concatenate([cosine] * 4, axis=1),
        jnp.concatenate([-sine, sine] * 2, axis=1),
    )


def ring(values, axis, step, size=4):
    return lax.ppermute(values, axis, [(i, (i + step) % size) for i in range(size)])


def swap(values):
    return lax.ppermute(values, "c", [(0, 1), (1, 0)])


def rolled(stack, start):
    return lax.dynamic_slice_in_dim(jnp.concatenate([stack, stack], axis=0), start, stack.shape[0], 0)


def along(block, axis):
    return [block] + [ring(block, axis, k) for k in range(1, 4)]


def back_along(chunks, axis):
    return [chunks[0]] + [ring(chunks[k], axis, 4 - k) for k in range(1, 4)]


def exchange(values, flip):
    pairs = [(2 * a + b, 2 * ((1 - b) if flip else b) + a) for a in range(2) for b in range(2)]
    return lax.ppermute(values, ("zl", "c"), pairs)


def exchange_back(values, flip):
    pairs = [(2 * a + b, 2 * b + ((1 - a) if flip else a)) for a in range(2) for b in range(2)]
    return lax.ppermute(values, ("zl", "c"), pairs)


def gather_column(shards, spot):
    w_query, w_key, w_value, w_out, w_gate, w_up, w_down, gain_attn, gain_ffn = shards
    first, even = spot["core"] == 0, spot["zl"] == 0

    def half(a_part, left, right):
        gains = jnp.concatenate([gain_attn, gain_ffn, jnp.zeros((252,), BF16)])[None]
        rows = jnp.concatenate([a_part, left, right], axis=1)
        return jnp.concatenate([rows, gains, jnp.zeros((5, 288), BF16)], axis=0)

    lower, upper = half(w_gate, w_query, w_key), half(w_up, w_out, w_value)
    keep = jnp.where(first, lower, upper)
    taken = swap(jnp.where(first, upper, lower))
    straight, flipped = exchange(w_down, False), exchange(w_down, True)
    pair = jnp.concatenate(
        [jnp.where(first, keep, taken), jnp.where(first, taken, keep)], axis=1
    )
    across = lax.ppermute(pair, "zl", [(0, 1), (1, 0)])
    both = jnp.concatenate(
        [jnp.where(even, pair, across), jnp.where(even, across, pair)], axis=0
    )
    down = jnp.concatenate(
        [jnp.where(even, straight, flipped), jnp.where(even, flipped, straight)], axis=1
    )
    column = along(jnp.concatenate([both, down], axis=1), "zh")
    stack = rolled(jnp.stack([column[k] for k in (0, 3, 2, 1)]), lax.rem(4 - spot["zh"], 4))
    upper_rows = stack[:, :, :576].reshape(4, 2, 24, 2, 288)

    def wide(part):
        return jnp.transpose(part[:, :, :18], (1, 2, 0, 3, 4)).reshape(36, -1)

    a_block = jnp.pad(wide(upper_rows[..., :192]), ((0, 4), (0, 0)))
    t_rows = jnp.concatenate(
        [wide(upper_rows[..., 192:264]), wide(upper_rows[..., 264:288])], axis=1
    )
    gain_rows = jnp.pad(upper_rows[0, :, 18, 0, :36], ((0, 2), (0, 768 - 36)))
    d_rows = jnp.transpose(stack[:, :, 576:].reshape(4, 48, 2, 72), (1, 0, 2, 3)).reshape(48, D)
    d_rows = jnp.pad(d_rows, ((0, 0), (0, 768 - D)))
    return a_block, jnp.concatenate([t_rows, gain_rows, d_rows], axis=0)


def gather_planes(a_block, b_block):
    a_parts, b_parts = along(a_block, "y"), along(b_block, "x")
    a_block = jnp.concatenate(a_parts, axis=0)
    b_block = jnp.concatenate(
        [part[:BLOCK_K] for part in b_parts] + [part[BLOCK_K:] for part in b_parts], axis=0
    )
    a_block, b_block = lax.optimization_barrier((a_block, b_block))
    mine_a, mine_b = along(a_block, "x"), along(b_block, "y")
    other_a, other_b = [swap(part) for part in mine_a], [swap(part) for part in mine_b]
    return (*mine_a, *other_a, *mine_b, *other_b)


def reduce_grads(results, spot):
    first, even = spot["core"] == 0, spot["zl"] == 0
    mine_a, other_a, mine_b, other_b = results[:4], results[4], results[5:9], results[9]
    pair_a, pair_b = run_pair(mine_a, swap(other_a)), run_pair(mine_b, swap(other_b))
    a_parts = run_stage(back_along(pair_a, "x"))
    b_parts = run_stage(back_along(pair_b, "y"))
    a_block = total(back_along(a_parts, "y")).astype(BF16)
    b_block = total(back_along(b_parts, "x")).astype(BF16)

    def narrow(part, width):
        return jnp.transpose(part.reshape(2, 18, 4, 2, width), (2, 0, 1, 3, 4))

    rows = jnp.concatenate(
        [narrow(a_block[:36], 192), narrow(b_block[:36, :D], 72), narrow(b_block[:36, D:], 24)],
        axis=-1,
    )
    gain_rows = jnp.broadcast_to(b_block[36:38, :36][None, :, None, None], (4, 2, 1, 2, 36))
    gain_rows = jnp.pad(gain_rows, ((0, 0), (0, 0), (0, 5), (0, 0), (0, 252)))
    rows = jnp.concatenate([rows, gain_rows], axis=2).reshape(4, 48, 576)
    down = jnp.transpose(b_block[BLOCK_K:, :D].reshape(48, 4, 144), (1, 0, 2))
    packets = rolled(jnp.concatenate([rows, down], axis=-1), spot["zh"])
    received = [packets[0]] + [ring(packets[k], "zh", k) for k in range(1, 4)]
    stack = rolled(jnp.stack([received[k] for k in (0, 3, 2, 1)]), lax.rem(4 - spot["zh"], 4))
    summed = jnp.sum(stack.astype(F32), axis=0)
    rows, down = summed[:, :576], summed[:, 576:]
    here = jnp.where(even, rows[:24], rows[24:])
    away = jnp.where(even, rows[24:], rows[:24]).astype(BF16)
    here = here + lax.ppermute(away, "zl", [(0, 1), (1, 0)]).astype(F32)
    down_low = down.astype(BF16)
    straight = exchange_back(jnp.where(even, down_low[:, :72], down_low[:, 72:]), False)
    flipped = exchange_back(jnp.where(even, down_low[:, 72:], down_low[:, :72]), True)
    low_half, high_half = here[:, :288], here[:, 288:]
    keep = jnp.where(first, low_half, high_half)
    taken = swap(jnp.where(first, high_half, low_half).astype(BF16)).astype(F32)
    lower = jnp.where(first, keep, taken)
    upper = jnp.where(first, taken, keep)
    gains = here[18]
    return (
        gains[:18],
        lower[:18, 192:264],
        lower[:18, 264:288],
        upper[:18, 264:288],
        upper[:18, 192:264],
        gains[18:36],
        lower[:18, :192],
        upper[:18, :192],
        straight.astype(F32) + flipped.astype(F32),
    )


def body(
    tokens,
    lengths,
    gain_attn,
    w_query,
    w_key,
    w_value,
    w_out,
    gain_ffn,
    w_gate,
    w_up,
    w_down,
    cotangent,
):
    core, z_high, z_low = lax.axis_index("c"), lax.axis_index("zh"), lax.axis_index("zl")
    x_pos, y_pos = lax.axis_index("x"), lax.axis_index("y")
    spot = {"core": core, "zh": z_high, "zl": z_low}
    ctx_pos = z_high * 2 + core
    spot_array = jnp.stack([core, x_pos, y_pos, ctx_pos]).astype(jnp.int32)
    x_own = tokens.reshape(2 * STRETCH, D)
    x_all = lax.all_gather(x_own, ("zh", "c"), axis=0, tiled=True)
    shards = (w_query, w_key, w_value, w_out, w_gate, w_up, w_down, gain_attn, gain_ffn)
    a_block, b_block = gather_column(shards, spot)
    a_block, b_block, lengths, x_pos, y_pos, ctx_pos = lax.optimization_barrier(
        (a_block, b_block, lengths, x_pos, y_pos, ctx_pos)
    )
    pieces = gather_planes(a_block, b_block)

    key_places = jnp.arange(GROUP, dtype=jnp.int32)
    query_places = ctx_pos * STRETCH + jnp.arange(STRETCH, dtype=jnp.int32)
    made = [row_tables(lengths[m, 0], key_places, query_places) for m in range(2)]
    bias = jnp.stack([made[0][0], made[1][0]])

    def by_slot(index):
        parts = [made[m][index].reshape(8, 1, STRETCH, HEAD // 2) for m in range(2)]
        return jnp.concatenate(parts, axis=1).reshape(2 * GROUP, HEAD // 2)

    tables = (bias,) + rotary_tables(by_slot(1), by_slot(2))
    places, gain_maps = placements(x_pos, y_pos)
    results = run_layer(
        spot_array,
        x_all,
        cotangent.reshape(2 * STRETCH, D),
        tables,
        places,
        gain_maps,
        pieces,
    )
    block_out, d_middle, d_normed, d_pairs, w_pairs, gain = results[:6]
    own_pairs = lax.psum_scatter(d_pairs, ("zh", "c"), scatter_dimension=0, tiled=True)
    grads = reduce_grads(results[6:], spot)
    d_tokens = run_final(x_own, gain, w_pairs, d_middle, d_normed, own_pairs)
    return (
        block_out.reshape(2, STRETCH, D),
        d_tokens.reshape(2, STRETCH, D),
        *grads,
    )


def placements(x_pos, y_pos):
    feature = jnp.arange(D, dtype=jnp.int32)
    z, x, y, i = feature // 288, (feature // 72) % 4, (feature // 18) % 4, feature % 18
    x_rel, y_rel = lax.rem(x_pos + 4 - x, 4), lax.rem(y_pos + 4 - y, 4)
    start_a, start_b = (x_rel * 4 + y_rel) * BLOCK_K, (y_rel * 4 + x_rel) * BLOCK_K
    inside = z * 18 + i
    columns = jnp.arange(PAD_K, dtype=jnp.int32)
    place_a = ((start_a + inside)[:, None] == columns[None, :]).astype(BF16)
    place_b = ((start_b + inside)[:, None] == columns[None, :]).astype(BF16)
    place_bt = ((start_b + inside)[None, :] == columns[:, None]).astype(BF16)
    row_mask = ((start_b + 36 + z)[None, :] == columns[:, None]).astype(BF16)
    lanes = jnp.arange(LANES, dtype=jnp.int32)[None, :]
    lane_maps = jnp.stack([i[:, None] == lanes, (i + 18)[:, None] == lanes]).astype(BF16)
    return (place_a, place_b, place_bt), (row_mask, lane_maps)


def solution(mesh):
    split = Mesh(mesh.devices.reshape(2, 4, 4, 4, 2), ("zl", "x", "y", "zh", "c"))
    rows, columns = ("zl", "x", "y"), ("zh", "c")
    everywhere = P(None, rows + columns, None)
    matrix, vector = P(rows, columns), P(rows)
    in_specs = (
        everywhere,
        P(None, rows, None),
        vector,
        matrix,
        matrix,
        matrix,
        matrix,
        vector,
        matrix,
        matrix,
        matrix,
        everywhere,
    )
    out_specs = (
        everywhere,
        everywhere,
        vector,
        matrix,
        matrix,
        matrix,
        matrix,
        vector,
        matrix,
        matrix,
        matrix,
    )
    return jax.shard_map(body, mesh=split, in_specs=in_specs, out_specs=out_specs, check_vma=False)
```

```python
import jax
import jax.numpy as jnp
from jax import lax
from jax.experimental import pallas as pl
from jax.experimental.pallas import tpu as pltpu
from jax.sharding import Mesh
from jax.sharding import PartitionSpec as P

HEADS = 9
KV_HEADS = 3
HEAD = 64
D = 576
FF = 1536
GROUP = 1024
STRETCH = 128
LANES = 128
CHUNK = 256
FF_CHUNK = 512
PAD_K = 640
BLOCK_K = 40
EPSILON = 1e-05
ROPE_BASE = 100000.0
MASKED = -1e30
F32 = jnp.float32
BF16 = jnp.bfloat16


def mm(a, b):
    return lax.dot_general(a, b, (((1,), (0,)), ((), ())), preferred_element_type=F32)


def mm_nt(a, b):
    return lax.dot_general(a, b, (((1,), (1,)), ((), ())), preferred_element_type=F32)


def mm_tn(a, b):
    return lax.dot_general(a, b, (((0,), (0,)), ((), ())), preferred_element_type=F32)


def rotate_lanes(values, cosine, sine):
    parts = []
    lanes = lax.broadcasted_iota(jnp.int32, (values.shape[0], LANES), 1)
    early = lanes % HEAD < HEAD // 2
    for start in range(0, values.shape[1], LANES):
        part = values[:, start : start + LANES]
        parts.append(
            part * cosine
            + jnp.where(
                early,
                pltpu.roll(part, LANES - HEAD // 2, 1),
                pltpu.roll(part, HEAD // 2, 1),
            )
            * sine
        )
    return jnp.concatenate(parts, axis=1)


def unpermute(values, table):
    high = values.astype(BF16)
    low = (values - high.astype(F32)).astype(BF16)
    return mm_nt(high, table) + mm_nt(low, table)


def inverse_rms(values):
    return lax.rsqrt(jnp.mean(values * values, axis=-1, keepdims=True) + EPSILON)


def layer_kernel(
    spot_ref,
    x_ref,
    back_ref,
    bias_ref,
    cos_ref,
    sine_ref,
    place_a_ref,
    place_b_ref,
    place_bt_ref,
    rows_ref,
    lanes_ref,
    *refs,
):
    mine_a, other_a, mine_b, other_b = (refs[4 * i : 4 * i + 4] for i in range(4))
    out_ref, d_middle_ref, d_normed_ref, d_pairs_ref, w_pairs_ref, gain_ref = refs[16:22]
    g_mine_a, g_other_a, g_mine_b, g_other_b = refs[22:26], refs[26], refs[27:31], refs[31]
    (
        attn_w_ref,
        gate_w_ref,
        up_w_ref,
        down_w_ref,
        attn_w,
        normed,
        keys,
        values,
        probs,
        mixed,
        mixed_low,
        hidden_ref,
        d_gate_s,
        d_up_s,
        d_query,
        shared,
        sems,
    ) = refs[32:]
    attn_g, middle_ref = attn_w_ref, d_middle_ref
    core, x_pos, y_pos, ctx_pos = spot_ref[0], spot_ref[1], spot_ref[2], spot_ref[3]

    def fetch(query_part, out_part, gate_part, up_part):
        for k in range(4):
            rows = pl.ds(k * 160, 160)
            top = pl.ds(0, 160)
            pltpu.make_async_copy(
                query_part[k].at[top], attn_w_ref.at[rows, pl.ds(0, 768)], sems.at[0]
            ).start()
            pltpu.make_async_copy(
                out_part[k].at[top], attn_w_ref.at[rows, pl.ds(768, 768)], sems.at[0]
            ).start()
        for k in range(4):
            rows = pl.ds(k * 160, 160)
            pltpu.make_async_copy(gate_part[k], gate_w_ref.at[rows], sems.at[1]).start()
            pltpu.make_async_copy(up_part[k], up_w_ref.at[rows], sems.at[2]).start()

    @pl.when(core == 0)
    def _():
        fetch(mine_b, other_b, mine_a, other_a)

    @pl.when(core == 1)
    def _():
        fetch(other_b, mine_b, other_a, mine_a)

    def down_start(k, j, half):
        y_index, x_index = lax.rem(y_pos + 4 - k, 4), lax.rem(x_pos + 4 - j, 4)
        return pl.multiple_of((half * 16 + x_index * 4 + y_index) * 48, 16)

    for k in range(4):
        for j in range(4):
            source = pl.ds(160 + 48 * j, 48)
            pltpu.make_async_copy(
                mine_b[k].at[source], down_w_ref.at[pl.ds(down_start(k, j, core), 48)], sems.at[3]
            ).start()
            pltpu.make_async_copy(
                other_b[k].at[source],
                down_w_ref.at[pl.ds(down_start(k, j, 1 - core), 48)],
                sems.at[3],
            ).start()

    def put(owner, value, store_mine, store_other):
        @pl.when(core == owner)
        def _():
            for k in range(4):
                store_mine(k, value[k * 160 : (k + 1) * 160])

        @pl.when(core != owner)
        def _():
            for k in range(4):
                store_other(k, value[k * 160 : (k + 1) * 160])

    def put_a(owner, cols, value):
        def store_mine(k, part):
            g_mine_a[k][:, cols] = part

        def store_other(k, part):
            g_other_a[k * 160 : (k + 1) * 160, cols] = part

        put(owner, value, store_mine, store_other)

    def put_b(owner, cols, value):
        def store_mine(k, part):
            g_mine_b[k][:160, cols] = part

        def store_other(k, part):
            g_other_b[k * 352 : k * 352 + 160, cols] = part

        put(owner, value, store_mine, store_other)

    pltpu.make_async_copy(attn_w_ref, attn_w_ref, sems.at[0]).wait()
    groups = HEADS // KV_HEADS
    own = 2 * STRETCH
    chunks = 2 * GROUP // CHUNK
    gain_rows = attn_w_ref[:, :LANES]
    row_mask = rows_ref[...].astype(F32)
    gain_attn = jnp.sum(mm_nt(gain_rows, lanes_ref[0]) * row_mask, axis=0, keepdims=True)
    gain_ffn = jnp.sum(mm_nt(gain_rows, lanes_ref[1]) * row_mask, axis=0, keepdims=True)
    gain_column = jnp.sum(
        mm_tn(rows_ref[...], gain_rows) * lanes_ref[0].astype(F32), axis=1, keepdims=True
    )
    gain_ref[...] = gain_attn
    for start in range(0, FF, FF_CHUNK):
        cols = slice(start, start + FF_CHUNK)
        attn_w[:, cols] = mm(place_b_ref[...], attn_w_ref[:, cols]).astype(BF16)
    w_pairs_ref[:, :256] = attn_w[:, 512:768]
    w_pairs_ref[:, 256:] = attn_w[:, 1280:]

    def project(step, carry):
        rows = pl.ds(pl.multiple_of(step * CHUNK, CHUNK), CHUNK)
        x_rows = x_ref[rows, :].astype(F32)
        scaled = (x_rows * inverse_rms(x_rows) * gain_attn).astype(BF16)
        normed[rows, :] = scaled
        turned_keys = rotate_lanes(
            mm(scaled, attn_w[:, 512:768]), cos_ref[rows, :], sine_ref[rows, :]
        )
        keys[rows, :] = turned_keys.astype(BF16)
        values[rows, :] = mm(scaled, attn_w[:, 1280:]).astype(BF16)
        return carry

    lax.fori_loop(0, chunks, project, 0)

    own_slot = pl.ds(pl.multiple_of(ctx_pos * own, own), own)
    cos_own, sine_own = cos_ref[own_slot, :], sine_ref[own_slot, :]
    normed_own = normed[own_slot, :]
    scale = HEAD ** (-0.5)
    queries = rotate_lanes(mm(normed_own, attn_w[:, :640]), cos_own, sine_own)
    queries = (queries.astype(BF16).astype(F32) * scale).astype(BF16)

    def of_micro(ref, micro, group):
        lanes = slice(HEAD * (group + 1), HEAD * (group + 2))
        start = micro * STRETCH
        return jnp.concatenate(
            [ref[k * own + start : k * own + start + STRETCH, lanes] for k in range(8)], axis=0
        )

    def stacked(array, micro, group):
        rows = slice(micro * STRETCH, (micro + 1) * STRETCH)
        return jnp.concatenate(
            [
                array[rows, HEAD * (group * groups + j) : HEAD * (1 + group * groups + j)]
                for j in range(groups)
            ],
            axis=0,
        )

    for micro in range(2):
        bias = bias_ref[micro]
        bias = jnp.concatenate([bias] * groups, axis=0)
        for group in range(KV_HEADS):
            key_rows = of_micro(keys, micro, group)
            value_rows = of_micro(values, micro, group)
            scores = mm_nt(stacked(queries, micro, group), key_rows) + bias
            weights = jnp.exp(scores - jnp.max(scores, axis=-1, keepdims=True))
            total = jnp.sum(weights, axis=-1, keepdims=True)
            low_probs = (weights * (1.0 / total)).astype(BF16)
            probs[micro * KV_HEADS + group] = low_probs
            mix = mm(low_probs, value_rows)
            mixed[micro * KV_HEADS + group] = mix
            for j in range(groups):
                head = group * groups + j
                mixed_low[
                    micro * STRETCH : (micro + 1) * STRETCH, HEAD * head : HEAD * (head + 1)
                ] = mix[j * STRETCH : (j + 1) * STRETCH].astype(BF16)

    x_own = x_ref[own_slot, :].astype(F32)
    middle = x_own + mm(mixed_low[...], attn_w[:, 768:1344])
    middle_ref[...] = middle
    scale_ffn = inverse_rms(middle)
    normed_ffn = mm((middle * scale_ffn * gain_ffn).astype(BF16), place_a_ref[...]).astype(BF16)
    back = back_ref[...]
    pltpu.make_async_copy(gate_w_ref, gate_w_ref, sems.at[1]).wait()
    pltpu.make_async_copy(up_w_ref, up_w_ref, sems.at[2]).wait()
    pltpu.make_async_copy(down_w_ref, down_w_ref, sems.at[3]).wait()
    for start in range(0, FF, FF_CHUNK):
        cols = slice(start, start + FF_CHUNK)
        gate = mm(normed_ffn, gate_w_ref[:, cols])
        up = mm(normed_ffn, up_w_ref[:, cols])
        sig = 1.0 / (1.0 + jnp.exp(-gate))
        silu = gate * sig
        hidden_ref[:, cols] = (silu * up).astype(BF16)
        d_hidden = mm_nt(back, down_w_ref[cols, :D])
        d_gate_s[:, cols] = (d_hidden * up * (sig + silu * (1.0 - sig))).astype(BF16)
        d_up_s[:, cols] = (d_hidden * silu).astype(BF16)
    hidden = hidden_ref[...]
    out_ref[...] = (middle + mm(hidden, down_w_ref[:, :D])).astype(BF16)
    d_rows = jnp.zeros((2 * STRETCH, PAD_K), F32)
    for start in range(0, FF, FF_CHUNK):
        cols = slice(start, start + FF_CHUNK)
        d_gate, d_up = d_gate_s[:, cols], d_up_s[:, cols]
        shared[cols, :D] = mm_tn(hidden_ref[:, cols], back)
        put_a(0, cols, mm_tn(normed_ffn, d_gate).astype(BF16))
        put_a(1, cols, mm_tn(normed_ffn, d_up).astype(BF16))
        d_rows = d_rows + mm_nt(d_gate, gate_w_ref[:, cols]) + mm_nt(d_up, up_w_ref[:, cols])
    d_normed_ffn = unpermute(d_rows, place_a_ref[...])
    middle = middle_ref[...]
    g_gain_ffn = jnp.sum(d_normed_ffn * middle * scale_ffn, axis=0, keepdims=True)
    d_scaled = d_normed_ffn * gain_ffn
    d_middle = (
        back.astype(F32)
        + scale_ffn * d_scaled
        - middle * scale_ffn**3 * jnp.mean(d_scaled * middle, axis=-1, keepdims=True)
    )
    d_middle_ref[...] = d_middle
    d_branch = d_middle.astype(BF16)
    attn_g[:D, 768:1344] = mm_tn(mixed_low[...], d_branch).astype(BF16)
    d_mixed = mm_nt(d_branch, attn_w[:, 768:1344]).astype(BF16)

    for k in range(4):
        for j in range(4):
            start = 160 + 48 * j
            g_mine_b[k][start : start + 48, :D] = shared[
                pl.ds(down_start(k, j, core), 48), :D
            ].astype(BF16)
            g_other_b[k * 352 + start : k * 352 + start + 48, :D] = shared[
                pl.ds(down_start(k, j, 1 - core), 48), :D
            ].astype(BF16)
        g_mine_b[k][160:, D:] = jnp.zeros((192, 768 - D), BF16)
        g_other_b[k * 352 + 160 : (k + 1) * 352, D:] = jnp.zeros((192, 768 - D), BF16)

    d_query[...] = jnp.zeros_like(d_query)
    shared[...] = jnp.zeros_like(shared)
    for micro in range(2):
        own_part = slice(micro * STRETCH, (micro + 1) * STRETCH)
        for group in range(KV_HEADS):
            key_rows = of_micro(keys, micro, group)
            value_rows = of_micro(values, micro, group)
            d_mix = jnp.concatenate(
                [
                    d_mixed[
                        own_part, HEAD * (group * groups + j) : HEAD * (group * groups + j + 1)
                    ]
                    for j in range(groups)
                ],
                axis=0,
            )
            delta = jnp.sum(
                d_mix.astype(F32) * mixed[micro * KV_HEADS + group], axis=-1, keepdims=True
            )
            low_probs = probs[micro * KV_HEADS + group]
            d_probs = mm_nt(d_mix, value_rows)
            d_scores = (low_probs.astype(F32) * (d_probs - delta)).astype(BF16)
            d_rows = mm(d_scores, key_rows) * scale
            for j in range(groups):
                head = group * groups + j
                d_query[own_part, HEAD * head : HEAD * (head + 1)] = d_rows[
                    j * STRETCH : (j + 1) * STRETCH
                ]
            d_key_rows = mm_tn(d_scores, stacked(queries, micro, group))
            d_value_rows = mm_tn(low_probs, d_mix)
            left, right = HEAD * (group + 1), 256 + HEAD * (group + 1)
            for k in range(8):
                rows = slice(k * own + micro * STRETCH, k * own + (micro + 1) * STRETCH)
                part = slice(k * STRETCH, (k + 1) * STRETCH)
                shared[rows, left : left + HEAD] = d_key_rows[part]
                shared[rows, right : right + HEAD] = d_value_rows[part]

    d_query_low = rotate_lanes(d_query[...], cos_own, -sine_own).astype(BF16)
    g_query = mm_tn(normed_own, d_query_low)
    d_normed = mm_nt(d_query_low, attn_w[:, :640])
    d_normed_ref[...] = d_normed

    def finish(step, carry):
        rows = pl.ds(pl.multiple_of(step * CHUNK, CHUNK), CHUNK)
        key_part = rotate_lanes(
            shared[rows, :256], cos_ref[rows, :], -sine_ref[rows, :]
        ).astype(BF16)
        value_part = shared[rows, 256:512].astype(BF16)
        d_pairs_ref[rows, :256] = key_part
        d_pairs_ref[rows, 256:] = value_part
        return carry

    lax.fori_loop(0, chunks, finish, 0)
    all_normed = normed[...]
    g_key = mm_tn(all_normed, d_pairs_ref[:, :256])
    g_value = mm_tn(all_normed, d_pairs_ref[:, 256:])
    attn_g[:D, :576] = g_query[:, :576].astype(BF16)
    attn_g[:D, 576:768] = g_key[:, 64:].astype(BF16)
    attn_g[:D, 1344:1536] = g_value[:, 64:].astype(BF16)
    g_gain_attn = (
        jnp.sum(attn_w[:, :640].astype(F32) * g_query, axis=1, keepdims=True)
        + jnp.sum(attn_w[:, 512:768].astype(F32) * g_key, axis=1, keepdims=True)
        + jnp.sum(attn_w[:, 1280:].astype(F32) * g_value, axis=1, keepdims=True)
    ) / gain_column
    gain_block = mm(rows_ref[...], (g_gain_attn * lanes_ref[0].astype(F32)).astype(BF16)) + mm(
        (row_mask * g_gain_ffn).astype(BF16), lanes_ref[1]
    )
    for start in (0, 768):
        part = mm(place_bt_ref[...], attn_g[:D, start : start + 768])
        put_b(start // 768, slice(LANES, 768), part[:, LANES:].astype(BF16))
        put_b(start // 768, slice(0, LANES), (part[:, :LANES] + gain_block).astype(BF16))


def pair_kernel(mine_0, mine_1, mine_2, mine_3, other_ref, *outs):
    size = mine_0.shape[0]
    for k, mine in enumerate((mine_0, mine_1, mine_2, mine_3)):
        other = other_ref[k * size : (k + 1) * size, :]
        outs[k][...] = (mine[...].astype(F32) + other.astype(F32)).astype(BF16)


def stage_kernel(*refs):
    result = total([ref[...] for ref in refs[:4]])
    for k, out in enumerate(refs[4:]):
        part = result[k * BLOCK_K : (k + 1) * BLOCK_K]
        if out.shape[0] > BLOCK_K:
            part = jnp.concatenate([part, result[160 + 48 * k : 208 + 48 * k]], axis=0)
        out[...] = part.astype(BF16)


def join_kernel(*refs):
    parts = [ref[...].astype(F32) for ref in refs[:4]]
    tops = [part[:BLOCK_K] for part in parts]
    refs[4][...] = jnp.concatenate(tops + [part[BLOCK_K:] for part in parts], axis=0).astype(BF16)


def finish_kernel(spot_ref, keep_ref, taken_ref, straight_ref, flipped_ref, *outs):
    first = spot_ref[0] == 0
    keep, taken = keep_ref[...], taken_ref[...].astype(F32)
    lower, upper = jnp.where(first, keep, taken), jnp.where(first, taken, keep)
    rows = slice(0, 18)
    for out, part in zip(
        outs,
        (
            keep[18:19, :18],
            lower[rows, 192:264],
            lower[rows, 264:288],
            upper[rows, 264:288],
            upper[rows, 192:264],
            keep[18:19, 18:36],
            lower[rows, :192],
            upper[rows, :192],
            straight_ref[...].astype(F32) + flipped_ref[...].astype(F32),
        ),
        strict=True,
    ):
        out[...] = part


def total(parts):
    result = parts[0].astype(F32)
    for part in parts[1:]:
        result = result + part.astype(F32)
    return result


def final_kernel(x_ref, gain_ref, w_pairs_ref, d_middle_ref, d_normed_ref, d_pairs_ref, out_ref):
    x_rows = x_ref[...].astype(F32)
    scale = inverse_rms(x_rows)
    d_scaled = (d_normed_ref[...] + mm_nt(d_pairs_ref[...], w_pairs_ref[...])) * gain_ref[...]
    out_ref[...] = (
        d_middle_ref[...]
        + scale * d_scaled
        - x_rows * scale**3 * jnp.mean(d_scaled * x_rows, axis=-1, keepdims=True)
    )


def vmem_call(kernel, outs, scratch=(), flops=0, moved=0, specs=None, limit=16):
    return pl.pallas_call(
        kernel,
        out_shape=outs,
        **({} if specs is None else {"in_specs": specs}),
        scratch_shapes=list(scratch),
        compiler_params=pltpu.CompilerParams(vmem_limit_bytes=limit * 1024 * 1024),
        cost_estimate=pl.CostEstimate(flops=flops, bytes_accessed=moved, transcendentals=0),
    )


def run_layer(spot, x_all, back, tables, places, gain_maps, pieces):
    own = 2 * STRETCH
    full = 2 * GROUP
    shape = jax.ShapeDtypeStruct
    outs = (
        shape((own, D), BF16),
        shape((own, D), F32),
        shape((own, D), F32),
        shape((full, 512), BF16),
        shape((D, 512), BF16),
        shape((1, D), F32),
    )
    outs = outs + (shape((160, FF), BF16),) * 4 + (shape((640, FF), BF16),)
    outs = outs + (shape((352, 768), BF16),) * 4 + (shape((1408, 768), BF16),)
    scratch = (
        pltpu.VMEM((PAD_K, FF), BF16),
        pltpu.VMEM((PAD_K, FF), BF16),
        pltpu.VMEM((PAD_K, FF), BF16),
        pltpu.VMEM((FF, 768), BF16),
        pltpu.VMEM((D, FF), BF16),
        pltpu.VMEM((full, D), BF16),
        pltpu.VMEM((full, 256), BF16),
        pltpu.VMEM((full, 256), BF16),
        pltpu.VMEM((6, 3 * STRETCH, GROUP), BF16),
        pltpu.VMEM((6, 3 * STRETCH, HEAD), F32),
        pltpu.VMEM((own, D), BF16),
        pltpu.VMEM((own, FF), BF16),
        pltpu.VMEM((own, FF), BF16),
        pltpu.VMEM((own, FF), BF16),
        pltpu.VMEM((own, PAD_K), F32),
        pltpu.VMEM((full, PAD_K), F32),
        pltpu.SemaphoreType.DMA((4,)),
    )
    specs = [pl.BlockSpec(memory_space=pltpu.SMEM)]
    specs = specs + [pl.BlockSpec(memory_space=pltpu.VMEM)] * 10
    specs = specs + [pl.BlockSpec(memory_space=pl.ANY)] * 16
    return vmem_call(layer_kernel, outs, scratch, 15 * 10**9, 60 * 10**6, specs, 62)(
        spot, x_all, back, *tables, *places, *gain_maps, *pieces
    )


def run_pair(mine, other):
    outs = tuple(jax.ShapeDtypeStruct(part.shape, BF16) for part in mine)
    return vmem_call(pair_kernel, outs, (), 10**6, 6 * 10**6)(*mine, other)


def run_stage(parts):
    rows = parts[0].shape[0] // 4
    outs = (jax.ShapeDtypeStruct((rows, parts[0].shape[1]), BF16),) * 4
    return vmem_call(stage_kernel, outs, (), 10**6, 3 * 10**6)(*parts)


def run_join(parts):
    out = jax.ShapeDtypeStruct((352, 768), BF16)
    return vmem_call(join_kernel, out, (), 10**6, 2 * 10**6)(*parts)


def run_finish(spot, keep, taken, straight, flipped):
    sizes = ((1, 18), (18, 72), (18, 24), (18, 24), (18, 72), (1, 18), (18, 192), (18, 192), (48, 72))
    outs = tuple(jax.ShapeDtypeStruct(size, F32) for size in sizes)
    specs = [pl.BlockSpec(memory_space=pltpu.SMEM)] + [pl.BlockSpec(memory_space=pltpu.VMEM)] * 4
    grads = vmem_call(finish_kernel, outs, (), 10**5, 10**5, specs)(
        spot, keep, taken, straight, flipped
    )
    return tuple(part.reshape(18) if part.shape[0] == 1 else part for part in grads)


def run_final(*args):
    outs = jax.ShapeDtypeStruct((2 * STRETCH, D), F32)
    return vmem_call(final_kernel, outs, (), 3 * 10**8, 4 * 10**6)(*args)


def row_tables(doc_sizes, key_places, query_places):
    ends = jnp.cumsum(doc_sizes)

    def start_of(places):
        passed = places[:, None] >= ends[None, :]
        return jnp.sum(jnp.where(passed, doc_sizes[None, :], 0), axis=1)

    starts = start_of(query_places)
    allowed = (key_places[None, :] >= starts[:, None]) & (
        key_places[None, :] <= query_places[:, None]
    )
    bias = jnp.where(allowed, 0.0, MASKED).astype(F32)
    positions = key_places - start_of(key_places)
    half = HEAD // 2
    frequencies = ROPE_BASE ** (-jnp.arange(half, dtype=F32) / half)
    angles = positions.astype(F32)[:, None] * frequencies[None, :]
    return bias, jnp.cos(angles), jnp.sin(angles)


def rotary_tables(cosine, sine):
    return (
        jnp.concatenate([cosine] * 4, axis=1),
        jnp.concatenate([-sine, sine] * 2, axis=1),
    )


def ring(values, axis, step, size=4):
    return lax.ppermute(values, axis, [(i, (i + step) % size) for i in range(size)])


def swap(values):
    return lax.ppermute(values, "c", [(0, 1), (1, 0)])


def rolled(stack, start):
    return lax.dynamic_slice_in_dim(jnp.concatenate([stack, stack], axis=0), start, stack.shape[0], 0)


def along(block, axis):
    return [block] + [ring(block, axis, k) for k in range(1, 4)]


def back_along(chunks, axis):
    return [chunks[0]] + [ring(chunks[k], axis, 4 - k) for k in range(1, 4)]


def exchange(values, flip):
    pairs = [(2 * a + b, 2 * ((1 - b) if flip else b) + a) for a in range(2) for b in range(2)]
    return lax.ppermute(values, ("zl", "c"), pairs)


def exchange_back(values, flip):
    pairs = [(2 * a + b, 2 * b + ((1 - a) if flip else a)) for a in range(2) for b in range(2)]
    return lax.ppermute(values, ("zl", "c"), pairs)


def gather_column(shards, spot):
    w_query, w_key, w_value, w_out, w_gate, w_up, w_down, gain_attn, gain_ffn = shards
    first, even = spot["core"] == 0, spot["zl"] == 0

    def half(a_part, left, right):
        gains = jnp.concatenate([gain_attn, gain_ffn, jnp.zeros((252,), BF16)])[None]
        rows = jnp.concatenate([a_part, left, right], axis=1)
        return jnp.concatenate([rows, gains, jnp.zeros((5, 288), BF16)], axis=0)

    lower, upper = half(w_gate, w_query, w_key), half(w_up, w_out, w_value)
    keep = jnp.where(first, lower, upper)
    taken = swap(jnp.where(first, upper, lower))
    straight, flipped = exchange(w_down, False), exchange(w_down, True)
    pair = jnp.concatenate(
        [jnp.where(first, keep, taken), jnp.where(first, taken, keep)], axis=1
    )
    across = lax.ppermute(pair, "zl", [(0, 1), (1, 0)])
    both = jnp.concatenate(
        [jnp.where(even, pair, across), jnp.where(even, across, pair)], axis=0
    )
    down = jnp.concatenate(
        [jnp.where(even, straight, flipped), jnp.where(even, flipped, straight)], axis=1
    )
    column = along(jnp.concatenate([both, down], axis=1), "zh")
    stack = rolled(jnp.stack([column[k] for k in (0, 3, 2, 1)]), lax.rem(4 - spot["zh"], 4))
    upper_rows = stack[:, :, :576].reshape(4, 2, 24, 2, 288)

    def wide(part):
        return jnp.transpose(part[:, :, :18], (1, 2, 0, 3, 4)).reshape(36, -1)

    a_block = jnp.pad(wide(upper_rows[..., :192]), ((0, 4), (0, 0)))
    t_rows = jnp.concatenate(
        [wide(upper_rows[..., 192:264]), wide(upper_rows[..., 264:288])], axis=1
    )
    gain_rows = jnp.pad(upper_rows[0, :, 18, 0, :36], ((0, 2), (0, 768 - 36)))
    d_rows = jnp.transpose(stack[:, :, 576:].reshape(4, 48, 2, 72), (1, 0, 2, 3)).reshape(48, D)
    d_rows = jnp.pad(d_rows, ((0, 0), (0, 768 - D)))
    return a_block, jnp.concatenate([t_rows, gain_rows, d_rows], axis=0)


def gather_planes(a_block, b_block, made):
    a_parts, b_parts = along(a_block, "y"), along(b_block, "x")
    a_block = jnp.concatenate(a_parts, axis=0)
    b_block = run_join(b_parts)
    a_block, b_block, made = lax.optimization_barrier((a_block, b_block, made))
    mine_a, mine_b = along(a_block, "x"), along(b_block, "y")
    other_a, other_b = [swap(part) for part in mine_a], [swap(part) for part in mine_b]
    return (*mine_a, *other_a, *mine_b, *other_b), made


def reduce_grads(results, spot, spot_array, own_pairs, finish):
    first, even = spot["core"] == 0, spot["zl"] == 0
    mine_a, other_a, mine_b, other_b = results[:4], results[4], results[5:9], results[9]
    pair_a, pair_b = run_pair(mine_a, swap(other_a)), run_pair(mine_b, swap(other_b))
    a_parts = run_stage(back_along(pair_a, "x"))
    b_parts = run_stage(back_along(pair_b, "y"))
    a_parts, b_parts, own_pairs = lax.optimization_barrier((a_parts, b_parts, own_pairs))
    d_tokens = finish(own_pairs)
    a_block = total(back_along(a_parts, "y")).astype(BF16)
    b_block = total(back_along(b_parts, "x")).astype(BF16)

    def narrow(part, width):
        return jnp.transpose(part.reshape(2, 18, 4, 2, width), (2, 0, 1, 3, 4))

    rows = jnp.concatenate(
        [narrow(a_block[:36], 192), narrow(b_block[:36, :D], 72), narrow(b_block[:36, D:], 24)],
        axis=-1,
    )
    gain_rows = jnp.broadcast_to(b_block[36:38, :36][None, :, None, None], (4, 2, 1, 2, 36))
    gain_rows = jnp.pad(gain_rows, ((0, 0), (0, 0), (0, 5), (0, 0), (0, 252)))
    rows = jnp.concatenate([rows, gain_rows], axis=2).reshape(4, 48, 576)
    down = jnp.transpose(b_block[BLOCK_K:, :D].reshape(48, 4, 144), (1, 0, 2))
    packets = rolled(jnp.concatenate([rows, down], axis=-1), spot["zh"])
    packets, d_tokens = lax.optimization_barrier((packets, d_tokens))
    received = [packets[0]] + [ring(packets[k], "zh", k) for k in range(1, 4)]
    stack = rolled(jnp.stack([received[k] for k in (0, 3, 2, 1)]), lax.rem(4 - spot["zh"], 4))
    summed = jnp.sum(stack.astype(F32), axis=0)
    rows, down = summed[:, :576], summed[:, 576:]
    here = jnp.where(even, rows[:24], rows[24:])
    away = jnp.where(even, rows[24:], rows[:24]).astype(BF16)
    here = here + lax.ppermute(away, "zl", [(0, 1), (1, 0)]).astype(F32)
    down_low = down.astype(BF16)
    straight = exchange_back(jnp.where(even, down_low[:, :72], down_low[:, 72:]), False)
    flipped = exchange_back(jnp.where(even, down_low[:, 72:], down_low[:, :72]), True)
    low_half, high_half = here[:, :288], here[:, 288:]
    keep = jnp.where(first, low_half, high_half)
    taken = swap(jnp.where(first, high_half, low_half).astype(BF16))
    return d_tokens, run_finish(spot_array, keep, taken, straight, flipped)


def body(
    tokens,
    lengths,
    gain_attn,
    w_query,
    w_key,
    w_value,
    w_out,
    gain_ffn,
    w_gate,
    w_up,
    w_down,
    cotangent,
):
    core, z_high, z_low = lax.axis_index("c"), lax.axis_index("zh"), lax.axis_index("zl")
    x_pos, y_pos = lax.axis_index("x"), lax.axis_index("y")
    spot = {"core": core, "zh": z_high, "zl": z_low}
    ctx_pos = z_high * 2 + core
    spot_array = jnp.stack([core, x_pos, y_pos, ctx_pos]).astype(jnp.int32)
    shards = (w_query, w_key, w_value, w_out, w_gate, w_up, w_down, gain_attn, gain_ffn)
    a_block, b_block = gather_column(shards, spot)
    x_own = tokens.reshape(2 * STRETCH, D)
    a_block, b_block, lengths, x_pos, y_pos, ctx_pos, x_own = lax.optimization_barrier(
        (a_block, b_block, lengths, x_pos, y_pos, ctx_pos, x_own)
    )
    x_all = lax.all_gather(x_own, ("zh", "c"), axis=0, tiled=True)
    key_places = jnp.arange(GROUP, dtype=jnp.int32)
    query_places = ctx_pos * STRETCH + jnp.arange(STRETCH, dtype=jnp.int32)
    made = [row_tables(lengths[m, 0], key_places, query_places) for m in range(2)]
    bias = jnp.stack([made[0][0], made[1][0]])

    def by_slot(index):
        parts = [made[m][index].reshape(8, 1, STRETCH, HEAD // 2) for m in range(2)]
        return jnp.concatenate(parts, axis=1).reshape(2 * GROUP, HEAD // 2)

    tables = (bias,) + rotary_tables(by_slot(1), by_slot(2))
    places, gain_maps = placements(x_pos, y_pos)
    pieces, (tables, places, gain_maps) = gather_planes(
        a_block, b_block, (tables, places, gain_maps)
    )
    results = run_layer(
        spot_array,
        x_all,
        cotangent.reshape(2 * STRETCH, D),
        tables,
        places,
        gain_maps,
        pieces,
    )
    block_out, d_middle, d_normed, d_pairs, w_pairs, gain = results[:6]
    own_pairs = lax.psum_scatter(d_pairs, ("zh", "c"), scatter_dimension=0, tiled=True)

    def finish(pairs):
        return run_final(x_own, gain, w_pairs, d_middle, d_normed, pairs)

    d_tokens, grads = reduce_grads(results[6:], spot, spot_array, own_pairs, finish)
    return (
        block_out.reshape(2, STRETCH, D),
        d_tokens.reshape(2, STRETCH, D),
        *grads,
    )


def placements(x_pos, y_pos):
    feature = jnp.arange(D, dtype=jnp.int32)
    z, x, y, i = feature // 288, (feature // 72) % 4, (feature // 18) % 4, feature % 18
    x_rel, y_rel = lax.rem(x_pos + 4 - x, 4), lax.rem(y_pos + 4 - y, 4)
    start_a, start_b = (x_rel * 4 + y_rel) * BLOCK_K, (y_rel * 4 + x_rel) * BLOCK_K
    inside = z * 18 + i
    columns = jnp.arange(PAD_K, dtype=jnp.int32)
    place_a = ((start_a + inside)[:, None] == columns[None, :]).astype(BF16)
    place_b = ((start_b + inside)[:, None] == columns[None, :]).astype(BF16)
    place_bt = ((start_b + inside)[None, :] == columns[:, None]).astype(BF16)
    row_mask = ((start_b + 36 + z)[None, :] == columns[:, None]).astype(BF16)
    lanes = jnp.arange(LANES, dtype=jnp.int32)[None, :]
    lane_maps = jnp.stack([i[:, None] == lanes, (i + 18)[:, None] == lanes]).astype(BF16)
    return (place_a, place_b, place_bt), (row_mask, lane_maps)


def solution(mesh):
    split = Mesh(mesh.devices.reshape(2, 4, 4, 4, 2), ("zl", "x", "y", "zh", "c"))
    rows, columns = ("zl", "x", "y"), ("zh", "c")
    everywhere = P(None, rows + columns, None)
    matrix, vector = P(rows, columns), P(rows)
    in_specs = (
        everywhere,
        P(None, rows, None),
        vector,
        matrix,
        matrix,
        matrix,
        matrix,
        vector,
        matrix,
        matrix,
        matrix,
        everywhere,
    )
    out_specs = (
        everywhere,
        everywhere,
        vector,
        matrix,
        matrix,
        matrix,
        matrix,
        vector,
        matrix,
        matrix,
        matrix,
    )
    return jax.shard_map(body, mesh=split, in_specs=in_specs, out_specs=out_specs, check_vma=False)
```

```python
import jax
import jax.numpy as jnp
from jax import lax
from jax.experimental import pallas as pl
from jax.experimental.pallas import tpu as pltpu
from jax.sharding import Mesh
from jax.sharding import PartitionSpec as P

HEADS = 9
KV_HEADS = 3
HEAD = 64
D = 576
FF = 1536
GROUP = 1024
STRETCH = 128
LANES = 128
CHUNK = 256
FF_CHUNK = 512
PAD_K = 640
BLOCK_K = 40
EPSILON = 1e-05
ROPE_BASE = 100000.0
MASKED = -1e30
F32 = jnp.float32
BF16 = jnp.bfloat16


def mm(a, b):
    return lax.dot_general(a, b, (((1,), (0,)), ((), ())), preferred_element_type=F32)


def mm_nt(a, b):
    return lax.dot_general(a, b, (((1,), (1,)), ((), ())), preferred_element_type=F32)


def mm_tn(a, b):
    return lax.dot_general(a, b, (((0,), (0,)), ((), ())), preferred_element_type=F32)


def rotate_lanes(values, cosine, sine):
    parts = []
    lanes = lax.broadcasted_iota(jnp.int32, (values.shape[0], LANES), 1)
    early = lanes % HEAD < HEAD // 2
    for start in range(0, values.shape[1], LANES):
        part = values[:, start : start + LANES]
        parts.append(
            part * cosine
            + jnp.where(
                early,
                pltpu.roll(part, LANES - HEAD // 2, 1),
                pltpu.roll(part, HEAD // 2, 1),
            )
            * sine
        )
    return jnp.concatenate(parts, axis=1)


def unpermute(values, table):
    high = values.astype(BF16)
    low = (values - high.astype(F32)).astype(BF16)
    return mm_nt(high, table) + mm_nt(low, table)


def inverse_rms(values):
    return lax.rsqrt(jnp.mean(values * values, axis=-1, keepdims=True) + EPSILON)


def layer_kernel(
    spot_ref,
    x_ref,
    back_ref,
    bias_ref,
    cos_ref,
    sine_ref,
    place_a_ref,
    place_b_ref,
    place_bt_ref,
    rows_ref,
    lanes_ref,
    *refs,
):
    mine_a, other_a, mine_b, other_b = (refs[4 * i : 4 * i + 4] for i in range(4))
    out_ref, d_middle_ref, d_normed_ref, d_pairs_ref, w_pairs_ref, gain_ref = refs[16:22]
    g_mine_a, g_other_a, g_mine_b, g_other_b = refs[22:26], refs[26], refs[27:31], refs[31]
    (
        attn_w_ref,
        gate_w_ref,
        up_w_ref,
        down_w_ref,
        attn_w,
        normed,
        keys,
        values,
        probs,
        mixed,
        mixed_low,
        hidden_ref,
        d_gate_s,
        d_up_s,
        d_query,
        shared,
        sems,
    ) = refs[32:]
    attn_g, middle_ref = attn_w_ref, d_middle_ref
    core, x_pos, y_pos, ctx_pos = spot_ref[0], spot_ref[1], spot_ref[2], spot_ref[3]

    def fetch(query_part, out_part, gate_part, up_part):
        for k in range(4):
            rows = pl.ds(k * 160, 160)
            top = pl.ds(0, 160)
            pltpu.make_async_copy(
                query_part[k].at[top], attn_w_ref.at[rows, pl.ds(0, 768)], sems.at[0]
            ).start()
            pltpu.make_async_copy(
                out_part[k].at[top], attn_w_ref.at[rows, pl.ds(768, 768)], sems.at[0]
            ).start()
        for k in range(4):
            rows = pl.ds(k * 160, 160)
            pltpu.make_async_copy(gate_part[k], gate_w_ref.at[rows], sems.at[1]).start()
            pltpu.make_async_copy(up_part[k], up_w_ref.at[rows], sems.at[2]).start()

    @pl.when(core == 0)
    def _():
        fetch(mine_b, other_b, mine_a, other_a)

    @pl.when(core == 1)
    def _():
        fetch(other_b, mine_b, other_a, mine_a)

    def down_start(k, j, half):
        y_index, x_index = lax.rem(y_pos + 4 - k, 4), lax.rem(x_pos + 4 - j, 4)
        return pl.multiple_of((half * 16 + x_index * 4 + y_index) * 48, 16)

    for k in range(4):
        for j in range(4):
            source = pl.ds(160 + 48 * j, 48)
            pltpu.make_async_copy(
                mine_b[k].at[source], down_w_ref.at[pl.ds(down_start(k, j, core), 48)], sems.at[3]
            ).start()
            pltpu.make_async_copy(
                other_b[k].at[source],
                down_w_ref.at[pl.ds(down_start(k, j, 1 - core), 48)],
                sems.at[3],
            ).start()

    def put(owner, value, store_mine, store_other):
        @pl.when(core == owner)
        def _():
            for k in range(4):
                store_mine(k, value[k * 160 : (k + 1) * 160])

        @pl.when(core != owner)
        def _():
            for k in range(4):
                store_other(k, value[k * 160 : (k + 1) * 160])

    def put_a(owner, cols, value):
        def store_mine(k, part):
            g_mine_a[k][:, cols] = part

        def store_other(k, part):
            g_other_a[k * 160 : (k + 1) * 160, cols] = part

        put(owner, value, store_mine, store_other)

    def put_b(owner, cols, value):
        def store_mine(k, part):
            g_mine_b[k][:160, cols] = part

        def store_other(k, part):
            g_other_b[k * 352 : k * 352 + 160, cols] = part

        put(owner, value, store_mine, store_other)

    pltpu.make_async_copy(attn_w_ref, attn_w_ref, sems.at[0]).wait()
    groups = HEADS // KV_HEADS
    own = 2 * STRETCH
    chunks = 2 * GROUP // CHUNK
    gain_rows = attn_w_ref[:, :LANES]
    row_mask = rows_ref[...].astype(F32)
    gain_attn = jnp.sum(mm_nt(gain_rows, lanes_ref[0]) * row_mask, axis=0, keepdims=True)
    gain_ffn = jnp.sum(mm_nt(gain_rows, lanes_ref[1]) * row_mask, axis=0, keepdims=True)
    gain_column = jnp.sum(
        mm_tn(rows_ref[...], gain_rows) * lanes_ref[0].astype(F32), axis=1, keepdims=True
    )
    gain_ref[...] = gain_attn
    for start in range(0, FF, FF_CHUNK):
        cols = slice(start, start + FF_CHUNK)
        attn_w[:, cols] = mm(place_b_ref[...], attn_w_ref[:, cols]).astype(BF16)
    w_pairs_ref[:, :256] = attn_w[:, 512:768]
    w_pairs_ref[:, 256:] = attn_w[:, 1280:]

    def project(step, carry):
        rows = pl.ds(pl.multiple_of(step * CHUNK, CHUNK), CHUNK)
        x_rows = x_ref[rows, :].astype(F32)
        scaled = (x_rows * inverse_rms(x_rows) * gain_attn).astype(BF16)
        normed[rows, :] = scaled
        turned_keys = rotate_lanes(
            mm(scaled, attn_w[:, 512:768]), cos_ref[rows, :], sine_ref[rows, :]
        )
        keys[rows, :] = turned_keys.astype(BF16)
        values[rows, :] = mm(scaled, attn_w[:, 1280:]).astype(BF16)
        return carry

    lax.fori_loop(0, chunks, project, 0)

    own_slot = pl.ds(pl.multiple_of(ctx_pos * own, own), own)
    cos_own, sine_own = cos_ref[own_slot, :], sine_ref[own_slot, :]
    normed_own = normed[own_slot, :]
    scale = HEAD ** (-0.5)
    queries = rotate_lanes(mm(normed_own, attn_w[:, :640]), cos_own, sine_own)
    queries = (queries.astype(BF16).astype(F32) * scale).astype(BF16)

    def of_micro(ref, micro, group):
        lanes = slice(HEAD * (group + 1), HEAD * (group + 2))
        start = micro * STRETCH
        return jnp.concatenate(
            [ref[k * own + start : k * own + start + STRETCH, lanes] for k in range(8)], axis=0
        )

    def stacked(array, micro, group):
        rows = slice(micro * STRETCH, (micro + 1) * STRETCH)
        return jnp.concatenate(
            [
                array[rows, HEAD * (group * groups + j) : HEAD * (1 + group * groups + j)]
                for j in range(groups)
            ],
            axis=0,
        )

    for micro in range(2):
        bias = bias_ref[micro]
        bias = jnp.concatenate([bias] * groups, axis=0)
        for group in range(KV_HEADS):
            key_rows = of_micro(keys, micro, group)
            value_rows = of_micro(values, micro, group)
            scores = mm_nt(stacked(queries, micro, group), key_rows) + bias
            weights = jnp.exp(scores - jnp.max(scores, axis=-1, keepdims=True))
            total = jnp.sum(weights, axis=-1, keepdims=True)
            low_probs = (weights * (1.0 / total)).astype(BF16)
            probs[micro * KV_HEADS + group] = low_probs
            mix = mm(low_probs, value_rows)
            mixed[micro * KV_HEADS + group] = mix
            for j in range(groups):
                head = group * groups + j
                mixed_low[
                    micro * STRETCH : (micro + 1) * STRETCH, HEAD * head : HEAD * (head + 1)
                ] = mix[j * STRETCH : (j + 1) * STRETCH].astype(BF16)

    x_own = x_ref[own_slot, :].astype(F32)
    middle = x_own + mm(mixed_low[...], attn_w[:, 768:1344])
    middle_ref[...] = middle
    scale_ffn = inverse_rms(middle)
    normed_ffn = mm((middle * scale_ffn * gain_ffn).astype(BF16), place_a_ref[...]).astype(BF16)
    back = back_ref[...]
    pltpu.make_async_copy(gate_w_ref, gate_w_ref, sems.at[1]).wait()
    pltpu.make_async_copy(up_w_ref, up_w_ref, sems.at[2]).wait()
    pltpu.make_async_copy(down_w_ref, down_w_ref, sems.at[3]).wait()
    for start in range(0, FF, FF_CHUNK):
        cols = slice(start, start + FF_CHUNK)
        gate = mm(normed_ffn, gate_w_ref[:, cols])
        up = mm(normed_ffn, up_w_ref[:, cols])
        sig = 1.0 / (1.0 + jnp.exp(-gate))
        silu = gate * sig
        hidden_ref[:, cols] = (silu * up).astype(BF16)
        d_hidden = mm_nt(back, down_w_ref[cols, :D])
        d_gate_s[:, cols] = (d_hidden * up * (sig + silu * (1.0 - sig))).astype(BF16)
        d_up_s[:, cols] = (d_hidden * silu).astype(BF16)
    hidden = hidden_ref[...]
    out_ref[...] = (middle + mm(hidden, down_w_ref[:, :D])).astype(BF16)
    d_rows = jnp.zeros((2 * STRETCH, PAD_K), F32)
    for start in range(0, FF, FF_CHUNK):
        cols = slice(start, start + FF_CHUNK)
        d_gate, d_up = d_gate_s[:, cols], d_up_s[:, cols]
        shared[cols, :D] = mm_tn(hidden_ref[:, cols], back)
        put_a(0, cols, mm_tn(normed_ffn, d_gate).astype(BF16))
        put_a(1, cols, mm_tn(normed_ffn, d_up).astype(BF16))
        d_rows = d_rows + mm_nt(d_gate, gate_w_ref[:, cols]) + mm_nt(d_up, up_w_ref[:, cols])
    d_normed_ffn = unpermute(d_rows, place_a_ref[...])
    middle = middle_ref[...]
    g_gain_ffn = jnp.sum(d_normed_ffn * middle * scale_ffn, axis=0, keepdims=True)
    d_scaled = d_normed_ffn * gain_ffn
    d_middle = (
        back.astype(F32)
        + scale_ffn * d_scaled
        - middle * scale_ffn**3 * jnp.mean(d_scaled * middle, axis=-1, keepdims=True)
    )
    d_middle_ref[...] = d_middle
    d_branch = d_middle.astype(BF16)
    attn_g[:D, 768:1344] = mm_tn(mixed_low[...], d_branch).astype(BF16)
    d_mixed = mm_nt(d_branch, attn_w[:, 768:1344]).astype(BF16)

    for k in range(4):
        for j in range(4):
            start = 160 + 48 * j
            g_mine_b[k][start : start + 48, :D] = shared[
                pl.ds(down_start(k, j, core), 48), :D
            ].astype(BF16)
            g_other_b[k * 352 + start : k * 352 + start + 48, :D] = shared[
                pl.ds(down_start(k, j, 1 - core), 48), :D
            ].astype(BF16)
        g_mine_b[k][160:, D:] = jnp.zeros((192, 768 - D), BF16)
        g_other_b[k * 352 + 160 : (k + 1) * 352, D:] = jnp.zeros((192, 768 - D), BF16)

    d_query[...] = jnp.zeros_like(d_query)
    shared[...] = jnp.zeros_like(shared)
    for micro in range(2):
        own_part = slice(micro * STRETCH, (micro + 1) * STRETCH)
        for group in range(KV_HEADS):
            key_rows = of_micro(keys, micro, group)
            value_rows = of_micro(values, micro, group)
            d_mix = jnp.concatenate(
                [
                    d_mixed[
                        own_part, HEAD * (group * groups + j) : HEAD * (group * groups + j + 1)
                    ]
                    for j in range(groups)
                ],
                axis=0,
            )
            delta = jnp.sum(
                d_mix.astype(F32) * mixed[micro * KV_HEADS + group], axis=-1, keepdims=True
            )
            low_probs = probs[micro * KV_HEADS + group]
            d_probs = mm_nt(d_mix, value_rows)
            d_scores = (low_probs.astype(F32) * (d_probs - delta)).astype(BF16)
            d_rows = mm(d_scores, key_rows) * scale
            for j in range(groups):
                head = group * groups + j
                d_query[own_part, HEAD * head : HEAD * (head + 1)] = d_rows[
                    j * STRETCH : (j + 1) * STRETCH
                ]
            d_key_rows = mm_tn(d_scores, stacked(queries, micro, group))
            d_value_rows = mm_tn(low_probs, d_mix)
            left, right = HEAD * (group + 1), 256 + HEAD * (group + 1)
            for k in range(8):
                rows = slice(k * own + micro * STRETCH, k * own + (micro + 1) * STRETCH)
                part = slice(k * STRETCH, (k + 1) * STRETCH)
                shared[rows, left : left + HEAD] = d_key_rows[part]
                shared[rows, right : right + HEAD] = d_value_rows[part]

    d_query_low = rotate_lanes(d_query[...], cos_own, -sine_own).astype(BF16)
    g_query = mm_tn(normed_own, d_query_low)
    d_normed = mm_nt(d_query_low, attn_w[:, :640])
    d_normed_ref[...] = d_normed

    def finish(step, carry):
        rows = pl.ds(pl.multiple_of(step * CHUNK, CHUNK), CHUNK)
        key_part = rotate_lanes(
            shared[rows, :256], cos_ref[rows, :], -sine_ref[rows, :]
        ).astype(BF16)
        value_part = shared[rows, 256:512].astype(BF16)
        d_pairs_ref[rows, :256] = key_part
        d_pairs_ref[rows, 256:] = value_part
        return carry

    lax.fori_loop(0, chunks, finish, 0)
    all_normed = normed[...]
    g_pairs = mm_tn(all_normed, d_pairs_ref[...])
    g_key, g_value = g_pairs[:, :256], g_pairs[:, 256:]
    attn_g[:D, :576] = g_query[:, :576].astype(BF16)
    attn_g[:D, 576:768] = g_key[:, 64:].astype(BF16)
    attn_g[:D, 1344:1536] = g_value[:, 64:].astype(BF16)
    g_gain_attn = (
        jnp.sum(attn_w[:, :640].astype(F32) * g_query, axis=1, keepdims=True)
        + jnp.sum(attn_w[:, 512:768].astype(F32) * g_key, axis=1, keepdims=True)
        + jnp.sum(attn_w[:, 1280:].astype(F32) * g_value, axis=1, keepdims=True)
    ) / gain_column
    gain_block = mm(rows_ref[...], (g_gain_attn * lanes_ref[0].astype(F32)).astype(BF16)) + mm(
        (row_mask * g_gain_ffn).astype(BF16), lanes_ref[1]
    )
    for start in (0, 768):
        part = mm(place_bt_ref[...], attn_g[:D, start : start + 768])
        put_b(start // 768, slice(LANES, 768), part[:, LANES:].astype(BF16))
        put_b(start // 768, slice(0, LANES), (part[:, :LANES] + gain_block).astype(BF16))


def pair_kernel(mine_0, mine_1, mine_2, mine_3, other_ref, *outs):
    size = mine_0.shape[0]
    for k, mine in enumerate((mine_0, mine_1, mine_2, mine_3)):
        other = other_ref[k * size : (k + 1) * size, :]
        outs[k][...] = (mine[...].astype(F32) + other.astype(F32)).astype(BF16)


def stage_kernel(*refs):
    result = total([ref[...] for ref in refs[:4]])
    for k, out in enumerate(refs[4:]):
        part = result[k * BLOCK_K : (k + 1) * BLOCK_K]
        if out.shape[0] > BLOCK_K:
            part = jnp.concatenate([part, result[160 + 48 * k : 208 + 48 * k]], axis=0)
        out[...] = part.astype(BF16)


def join_kernel(*refs):
    parts = [ref[...].astype(F32) for ref in refs[:4]]
    tops = [part[:BLOCK_K] for part in parts]
    refs[4][...] = jnp.concatenate(tops + [part[BLOCK_K:] for part in parts], axis=0).astype(BF16)


def finish_kernel(spot_ref, keep_ref, taken_ref, straight_ref, flipped_ref, *outs):
    first = spot_ref[0] == 0
    keep, taken = keep_ref[...], taken_ref[...].astype(F32)
    lower, upper = jnp.where(first, keep, taken), jnp.where(first, taken, keep)
    rows = slice(0, 18)
    for out, part in zip(
        outs,
        (
            keep[18:19, :18],
            lower[rows, 192:264],
            lower[rows, 264:288],
            upper[rows, 264:288],
            upper[rows, 192:264],
            keep[18:19, 18:36],
            lower[rows, :192],
            upper[rows, :192],
            straight_ref[...].astype(F32) + flipped_ref[...].astype(F32),
        ),
        strict=True,
    ):
        out[...] = part


def total(parts):
    result = parts[0].astype(F32)
    for part in parts[1:]:
        result = result + part.astype(F32)
    return result


def final_kernel(x_ref, gain_ref, w_pairs_ref, d_middle_ref, d_normed_ref, d_pairs_ref, out_ref):
    x_rows = x_ref[...].astype(F32)
    scale = inverse_rms(x_rows)
    d_scaled = (d_normed_ref[...] + mm_nt(d_pairs_ref[...], w_pairs_ref[...])) * gain_ref[...]
    out_ref[...] = (
        d_middle_ref[...]
        + scale * d_scaled
        - x_rows * scale**3 * jnp.mean(d_scaled * x_rows, axis=-1, keepdims=True)
    )


def vmem_call(kernel, outs, scratch=(), flops=0, moved=0, specs=None, limit=16):
    return pl.pallas_call(
        kernel,
        out_shape=outs,
        **({} if specs is None else {"in_specs": specs}),
        scratch_shapes=list(scratch),
        compiler_params=pltpu.CompilerParams(vmem_limit_bytes=limit * 1024 * 1024),
        cost_estimate=pl.CostEstimate(flops=flops, bytes_accessed=moved, transcendentals=0),
    )


def run_layer(spot, x_all, back, tables, places, gain_maps, pieces):
    own = 2 * STRETCH
    full = 2 * GROUP
    shape = jax.ShapeDtypeStruct
    outs = (
        shape((own, D), BF16),
        shape((own, D), F32),
        shape((own, D), F32),
        shape((full, 512), BF16),
        shape((D, 512), BF16),
        shape((1, D), F32),
    )
    outs = outs + (shape((160, FF), BF16),) * 4 + (shape((640, FF), BF16),)
    outs = outs + (shape((352, 768), BF16),) * 4 + (shape((1408, 768), BF16),)
    scratch = (
        pltpu.VMEM((PAD_K, FF), BF16),
        pltpu.VMEM((PAD_K, FF), BF16),
        pltpu.VMEM((PAD_K, FF), BF16),
        pltpu.VMEM((FF, 768), BF16),
        pltpu.VMEM((D, FF), BF16),
        pltpu.VMEM((full, D), BF16),
        pltpu.VMEM((full, 256), BF16),
        pltpu.VMEM((full, 256), BF16),
        pltpu.VMEM((6, 3 * STRETCH, GROUP), BF16),
        pltpu.VMEM((6, 3 * STRETCH, HEAD), F32),
        pltpu.VMEM((own, D), BF16),
        pltpu.VMEM((own, FF), BF16),
        pltpu.VMEM((own, FF), BF16),
        pltpu.VMEM((own, FF), BF16),
        pltpu.VMEM((own, PAD_K), F32),
        pltpu.VMEM((full, PAD_K), F32),
        pltpu.SemaphoreType.DMA((4,)),
    )
    specs = [pl.BlockSpec(memory_space=pltpu.SMEM)]
    specs = specs + [pl.BlockSpec(memory_space=pltpu.VMEM)] * 10
    specs = specs + [pl.BlockSpec(memory_space=pl.ANY)] * 16
    return vmem_call(layer_kernel, outs, scratch, 15 * 10**9, 60 * 10**6, specs, 62)(
        spot, x_all, back, *tables, *places, *gain_maps, *pieces
    )


def run_pair(mine, other):
    outs = tuple(jax.ShapeDtypeStruct(part.shape, BF16) for part in mine)
    return vmem_call(pair_kernel, outs, (), 10**6, 6 * 10**6)(*mine, other)


def run_stage(parts):
    rows = parts[0].shape[0] // 4
    outs = (jax.ShapeDtypeStruct((rows, parts[0].shape[1]), BF16),) * 4
    return vmem_call(stage_kernel, outs, (), 10**6, 3 * 10**6)(*parts)


def run_join(parts):
    out = jax.ShapeDtypeStruct((352, 768), BF16)
    return vmem_call(join_kernel, out, (), 10**6, 2 * 10**6)(*parts)


def run_finish(spot, keep, taken, straight, flipped):
    sizes = ((1, 18), (18, 72), (18, 24), (18, 24), (18, 72), (1, 18), (18, 192), (18, 192), (48, 72))
    outs = tuple(jax.ShapeDtypeStruct(size, F32) for size in sizes)
    specs = [pl.BlockSpec(memory_space=pltpu.SMEM)] + [pl.BlockSpec(memory_space=pltpu.VMEM)] * 4
    grads = vmem_call(finish_kernel, outs, (), 10**5, 10**5, specs)(
        spot, keep, taken, straight, flipped
    )
    return tuple(part.reshape(18) if part.shape[0] == 1 else part for part in grads)


def run_final(*args):
    outs = jax.ShapeDtypeStruct((2 * STRETCH, D), F32)
    return vmem_call(final_kernel, outs, (), 3 * 10**8, 4 * 10**6)(*args)


def row_tables(doc_sizes, key_places, query_places):
    ends = jnp.cumsum(doc_sizes)

    def start_of(places):
        passed = places[:, None] >= ends[None, :]
        return jnp.sum(jnp.where(passed, doc_sizes[None, :], 0), axis=1)

    starts = start_of(query_places)
    allowed = (key_places[None, :] >= starts[:, None]) & (
        key_places[None, :] <= query_places[:, None]
    )
    bias = jnp.where(allowed, 0.0, MASKED).astype(F32)
    positions = key_places - start_of(key_places)
    half = HEAD // 2
    frequencies = ROPE_BASE ** (-jnp.arange(half, dtype=F32) / half)
    angles = positions.astype(F32)[:, None] * frequencies[None, :]
    return bias, jnp.cos(angles), jnp.sin(angles)


def rotary_tables(cosine, sine):
    return (
        jnp.concatenate([cosine] * 4, axis=1),
        jnp.concatenate([-sine, sine] * 2, axis=1),
    )


def ring(values, axis, step, size=4):
    return lax.ppermute(values, axis, [(i, (i + step) % size) for i in range(size)])


def swap(values):
    return lax.ppermute(values, "c", [(0, 1), (1, 0)])


def rolled(stack, start):
    return lax.dynamic_slice_in_dim(jnp.concatenate([stack, stack], axis=0), start, stack.shape[0], 0)


def along(block, axis):
    return [block] + [ring(block, axis, k) for k in range(1, 4)]


def back_along(chunks, axis):
    return [chunks[0]] + [ring(chunks[k], axis, 4 - k) for k in range(1, 4)]


def exchange(values, flip):
    pairs = [(2 * a + b, 2 * ((1 - b) if flip else b) + a) for a in range(2) for b in range(2)]
    return lax.ppermute(values, ("zl", "c"), pairs)


def exchange_back(values, flip):
    pairs = [(2 * a + b, 2 * b + ((1 - a) if flip else a)) for a in range(2) for b in range(2)]
    return lax.ppermute(values, ("zl", "c"), pairs)


def gather_column(shards, spot):
    w_query, w_key, w_value, w_out, w_gate, w_up, w_down, gain_attn, gain_ffn = shards
    first, even = spot["core"] == 0, spot["zl"] == 0

    def half(a_part, left, right):
        gains = jnp.concatenate([gain_attn, gain_ffn, jnp.zeros((252,), BF16)])[None]
        rows = jnp.concatenate([a_part, left, right], axis=1)
        return jnp.concatenate([rows, gains, jnp.zeros((5, 288), BF16)], axis=0)

    lower, upper = half(w_gate, w_query, w_key), half(w_up, w_out, w_value)
    keep = jnp.where(first, lower, upper)
    taken = swap(jnp.where(first, upper, lower))
    straight, flipped = exchange(w_down, False), exchange(w_down, True)
    pair = jnp.concatenate(
        [jnp.where(first, keep, taken), jnp.where(first, taken, keep)], axis=1
    )
    across = lax.ppermute(pair, "zl", [(0, 1), (1, 0)])
    both = jnp.concatenate(
        [jnp.where(even, pair, across), jnp.where(even, across, pair)], axis=0
    )
    down = jnp.concatenate(
        [jnp.where(even, straight, flipped), jnp.where(even, flipped, straight)], axis=1
    )
    column = along(jnp.concatenate([both, down], axis=1), "zh")
    stack = rolled(jnp.stack([column[k] for k in (0, 3, 2, 1)]), lax.rem(4 - spot["zh"], 4))
    upper_rows = stack[:, :, :576].reshape(4, 2, 24, 2, 288)

    def wide(part):
        return jnp.transpose(part[:, :, :18], (1, 2, 0, 3, 4)).reshape(36, -1)

    a_block = jnp.pad(wide(upper_rows[..., :192]), ((0, 4), (0, 0)))
    t_rows = jnp.concatenate(
        [wide(upper_rows[..., 192:264]), wide(upper_rows[..., 264:288])], axis=1
    )
    gain_rows = jnp.pad(upper_rows[0, :, 18, 0, :36], ((0, 2), (0, 768 - 36)))
    d_rows = jnp.transpose(stack[:, :, 576:].reshape(4, 48, 2, 72), (1, 0, 2, 3)).reshape(48, D)
    d_rows = jnp.pad(d_rows, ((0, 0), (0, 768 - D)))
    return a_block, jnp.concatenate([t_rows, gain_rows, d_rows], axis=0)


def gather_planes(a_block, b_block, seeds, make):
    a_parts, b_parts = along(a_block, "y"), along(b_block, "x")
    a_block = jnp.concatenate(a_parts, axis=0)
    b_block = run_join(b_parts)
    a_block, b_block, seeds = lax.optimization_barrier((a_block, b_block, seeds))
    made = make(*seeds)
    mine_a, mine_b = along(a_block, "x"), along(b_block, "y")
    mine_a[3], mine_a[0], made = lax.optimization_barrier((mine_a[3], mine_a[0], made))
    mine_b[3], mine_b[0] = lax.optimization_barrier((mine_b[3], mine_b[0]))
    other_a, other_b = [swap(part) for part in mine_a], [swap(part) for part in mine_b]
    return (*mine_a, *other_a, *mine_b, *other_b), made


def reduce_grads(results, spot, spot_array, own_pairs, finish):
    first, even = spot["core"] == 0, spot["zl"] == 0
    mine_a, other_a, mine_b, other_b = results[:4], results[4], results[5:9], results[9]
    pair_a, pair_b = run_pair(mine_a, swap(other_a)), run_pair(mine_b, swap(other_b))
    a_parts = run_stage(back_along(pair_a, "x"))
    b_parts = run_stage(back_along(pair_b, "y"))
    a_parts, b_parts, own_pairs = lax.optimization_barrier((a_parts, b_parts, own_pairs))
    d_tokens = finish(own_pairs)
    a_block = total(back_along(a_parts, "y")).astype(BF16)
    b_block = total(back_along(b_parts, "x")).astype(BF16)

    def narrow(part, width):
        return jnp.transpose(part.reshape(2, 18, 4, 2, width), (2, 0, 1, 3, 4))

    rows = jnp.concatenate(
        [narrow(a_block[:36], 192), narrow(b_block[:36, :D], 72), narrow(b_block[:36, D:], 24)],
        axis=-1,
    )
    gain_rows = jnp.broadcast_to(b_block[36:38, :36][None, :, None, None], (4, 2, 1, 2, 36))
    gain_rows = jnp.pad(gain_rows, ((0, 0), (0, 0), (0, 5), (0, 0), (0, 252)))
    rows = jnp.concatenate([rows, gain_rows], axis=2).reshape(4, 48, 576)
    down = jnp.transpose(b_block[BLOCK_K:, :D].reshape(48, 4, 144), (1, 0, 2))
    packets = rolled(jnp.concatenate([rows, down], axis=-1), spot["zh"])
    packets, d_tokens = lax.optimization_barrier((packets, d_tokens))
    received = [packets[0]] + [ring(packets[k], "zh", k) for k in range(1, 4)]
    stack = rolled(jnp.stack([received[k] for k in (0, 3, 2, 1)]), lax.rem(4 - spot["zh"], 4))
    summed = jnp.sum(stack.astype(F32), axis=0)
    rows, down = summed[:, :576], summed[:, 576:]
    here = jnp.where(even, rows[:24], rows[24:])
    away = jnp.where(even, rows[24:], rows[:24]).astype(BF16)
    here = here + lax.ppermute(away, "zl", [(0, 1), (1, 0)]).astype(F32)
    down_low = down.astype(BF16)
    straight = exchange_back(jnp.where(even, down_low[:, :72], down_low[:, 72:]), False)
    flipped = exchange_back(jnp.where(even, down_low[:, 72:], down_low[:, :72]), True)
    low_half, high_half = here[:, :288], here[:, 288:]
    keep = jnp.where(first, low_half, high_half)
    taken = swap(jnp.where(first, high_half, low_half).astype(BF16))
    return d_tokens, run_finish(spot_array, keep, taken, straight, flipped)


def position_tables(lengths, x_pos, y_pos, ctx_pos):
    key_places = jnp.arange(GROUP, dtype=jnp.int32)
    query_places = ctx_pos * STRETCH + jnp.arange(STRETCH, dtype=jnp.int32)
    made = [row_tables(lengths[m, 0], key_places, query_places) for m in range(2)]
    bias = jnp.stack([made[0][0], made[1][0]])

    def by_slot(index):
        parts = [made[m][index].reshape(8, 1, STRETCH, HEAD // 2) for m in range(2)]
        return jnp.concatenate(parts, axis=1).reshape(2 * GROUP, HEAD // 2)

    tables = (bias,) + rotary_tables(by_slot(1), by_slot(2))
    places, gain_maps = placements(x_pos, y_pos)
    return tables, places, gain_maps


def body(
    tokens,
    lengths,
    gain_attn,
    w_query,
    w_key,
    w_value,
    w_out,
    gain_ffn,
    w_gate,
    w_up,
    w_down,
    cotangent,
):
    core, z_high, z_low = lax.axis_index("c"), lax.axis_index("zh"), lax.axis_index("zl")
    x_pos, y_pos = lax.axis_index("x"), lax.axis_index("y")
    spot = {"core": core, "zh": z_high, "zl": z_low}
    ctx_pos = z_high * 2 + core
    spot_array = jnp.stack([core, x_pos, y_pos, ctx_pos]).astype(jnp.int32)
    shards = (w_query, w_key, w_value, w_out, w_gate, w_up, w_down, gain_attn, gain_ffn)
    a_block, b_block = gather_column(shards, spot)
    x_own = tokens.reshape(2 * STRETCH, D)
    a_block, b_block, lengths, x_pos, y_pos, ctx_pos, x_own = lax.optimization_barrier(
        (a_block, b_block, lengths, x_pos, y_pos, ctx_pos, x_own)
    )
    x_all = lax.all_gather(x_own, ("zh", "c"), axis=0, tiled=True)
    pieces, (tables, places, gain_maps) = gather_planes(
        a_block, b_block, (lengths, x_pos, y_pos, ctx_pos), position_tables
    )
    results = run_layer(
        spot_array,
        x_all,
        cotangent.reshape(2 * STRETCH, D),
        tables,
        places,
        gain_maps,
        pieces,
    )
    block_out, d_middle, d_normed, d_pairs, w_pairs, gain = results[:6]
    own_pairs = lax.psum_scatter(d_pairs, ("zh", "c"), scatter_dimension=0, tiled=True)

    def finish(pairs):
        return run_final(x_own, gain, w_pairs, d_middle, d_normed, pairs)

    d_tokens, grads = reduce_grads(results[6:], spot, spot_array, own_pairs, finish)
    return (
        block_out.reshape(2, STRETCH, D),
        d_tokens.reshape(2, STRETCH, D),
        *grads,
    )


def placements(x_pos, y_pos):
    feature = jnp.arange(D, dtype=jnp.int32)
    z, x, y, i = feature // 288, (feature // 72) % 4, (feature // 18) % 4, feature % 18
    x_rel, y_rel = lax.rem(x_pos + 4 - x, 4), lax.rem(y_pos + 4 - y, 4)
    start_a, start_b = (x_rel * 4 + y_rel) * BLOCK_K, (y_rel * 4 + x_rel) * BLOCK_K
    inside = z * 18 + i
    columns = jnp.arange(PAD_K, dtype=jnp.int32)
    place_a = ((start_a + inside)[:, None] == columns[None, :]).astype(BF16)
    place_b = ((start_b + inside)[:, None] == columns[None, :]).astype(BF16)
    place_bt = ((start_b + inside)[None, :] == columns[:, None]).astype(BF16)
    row_mask = ((start_b + 36 + z)[None, :] == columns[:, None]).astype(BF16)
    lanes = jnp.arange(LANES, dtype=jnp.int32)[None, :]
    lane_maps = jnp.stack([i[:, None] == lanes, (i + 18)[:, None] == lanes]).astype(BF16)
    return (place_a, place_b, place_bt), (row_mask, lane_maps)


def solution(mesh):
    split = Mesh(mesh.devices.reshape(2, 4, 4, 4, 2), ("zl", "x", "y", "zh", "c"))
    rows, columns = ("zl", "x", "y"), ("zh", "c")
    everywhere = P(None, rows + columns, None)
    matrix, vector = P(rows, columns), P(rows)
    in_specs = (
        everywhere,
        P(None, rows, None),
        vector,
        matrix,
        matrix,
        matrix,
        matrix,
        vector,
        matrix,
        matrix,
        matrix,
        everywhere,
    )
    out_specs = (
        everywhere,
        everywhere,
        vector,
        matrix,
        matrix,
        matrix,
        matrix,
        vector,
        matrix,
        matrix,
        matrix,
    )
    return jax.shard_map(body, mesh=split, in_specs=in_specs, out_specs=out_specs, check_vma=False)
```
